32 devices in a mesh: leaf: 8 (over z, y), rhs: 4 (over x, core).
Axes of the slice: x: 2, y: 2, z: 4, core: 2. Of those that a mesh axis runs over, the one named last changes fastest.
Arguments:
- obs_coef: float32 [128, 2048], P('rhs', 'leaf'), may hold values from -0.75 to 0.75
- obs_data: float32 [320, 2048], P('rhs', 'leaf'), may hold values from -6 to 6
- obs_target: int32 [2048], P('leaf'), may hold values from 0 to 31, as said below
- leaf_map: int32 [32], replicated, may hold values from 0 to 31, as said below
- leaf_parent: int32 [32], replicated, may hold values from 0 to 7
- leaf_inv: float32 [32, 128, 128], P('leaf'), may hold values from -0.5 to 1.5
- leaf_off: float32 [32, 128, 128], P('leaf'), may hold values from -0.25 to 0.25
- top_inv: float32 [8, 128, 128], replicated, may hold values from -0.5 to 1.5
- top_rhs: float32 [8, 320, 128], P(None, 'rhs'), may hold values from -6 to 6
Outputs:
- leaf_solution: float32 [32, 320, 128], P('leaf', 'rhs')
- top_solution: float32 [8, 320, 128], P(None, 'rhs')
The draws below stay inside these ranges and needn't reach their ends.
Inputs may be any that keep to these rules, and one draw needn't show every extreme that they name: A permutation: supernode i is stored at position leaf_map[i], which lies on index leaf_map[i] // 4 of leaf. `obs_target`: the rows held by one index of leaf name supernodes stored on any one index of leaf at most 64 times; in every draw one index of leaf is named exactly 64 times by the rows of every index.
All inputs are finite; a program needn't handle non-finite values.
Results may differ from the reference program's by a relative error of at most 0.0003.
Values sent between devices are 32-bit elements; how exact they have to be, the bound alone decides.
A program may use at most 64 MiB of HBM per device.

```python
import math
import jax
import jax.numpy as jnp
from jax import lax

BLOCK = 128
DATES = 320
NTOP = 8
LEAF_DEV = 4
OBS_DEV = 256
NLEAF = 32
OBS = 2048
CAP = 64
N_LEAF = 8


def placement_draw(key):
    base_key = jax.random.fold_in(key, 7)
    key_map, key_hot, key_score, key_member, key_shuffle = jax.random.split(base_key, 5)
    devices = NLEAF // LEAF_DEV
    slots_all = devices * CAP
    leaf_map = jax.random.permutation(key_map, NLEAF).astype(jnp.int32)
    holder = jnp.argsort(leaf_map).astype(jnp.int32)
    hot_owner = jax.random.randint(key_hot, (), 0, devices, dtype=jnp.int32)
    slot_index = jnp.arange(slots_all, dtype=jnp.int32)
    slot_owner = slot_index // CAP
    scores = jax.random.randint(key_score, (devices, slots_all), 0, 2 ** 16, dtype=jnp.int32) * slots_all + slot_index[None, :]
    sort_keys = jnp.where(slot_owner[None, :] == hot_owner, 0, 2 ** 28) + scores
    taken = jnp.argsort(sort_keys, axis=1)[:, :OBS_DEV].astype(jnp.int32)
    dest_owner = taken // CAP
    dest_owner = jax.random.permutation(key_shuffle, dest_owner, axis=1, independent=True)
    member = jax.random.randint(key_member, (devices, OBS_DEV), 0, LEAF_DEV, dtype=jnp.int32)
    obs_target = holder[dest_owner * LEAF_DEV + member].reshape(-1).astype(jnp.int32)
    return (leaf_map, obs_target)


def draw_leaf_map(key, part):
    return placement_draw(key)[0]


def draw_obs_target(key, part):
    return placement_draw(key)[1]


def lower_blocks(key, count):
    key_diag, key_off = jax.random.split(key)
    row_index = jnp.arange(BLOCK)[:, None]
    col_index = jnp.arange(BLOCK)[None, :]
    below_diag = row_index > col_index
    on_diag = row_index == col_index
    diagonal = jnp.exp(jax.random.uniform(key_diag, (count, BLOCK, 1), jnp.float32, math.log(0.5), math.log(1.5)))
    off_diag = 0.08 * jnp.clip(jax.random.normal(key_off, (count, BLOCK, BLOCK), jnp.float32), -6.0, 6.0)
    return jnp.where(below_diag, off_diag, 0.0) + jnp.where(on_diag, diagonal, 0.0)


def draw_leaf_inv(key, part):
    return lower_blocks(jax.random.fold_in(key, 11), NLEAF)


def draw_top_inv(key, part):
    return lower_blocks(jax.random.fold_in(key, 13), NTOP)


def with_ends(values, key, smallest, top_value):
    spot = [jax.random.randint(jax.random.fold_in(key, axis), (), 0, length) for axis, length in enumerate(values.shape)]
    longest = values.shape.index(max(values.shape))
    neighbour = spot[:longest] + [(spot[longest] + 1) % values.shape[longest]] + spot[longest + 1:]
    return values.at[tuple(spot)].set(smallest).at[tuple(neighbour)].set(top_value)


def level_of(stream_key, extent, pieces, low, high):
    loudness = 1.0
    for axis_at, shards_of in pieces:
        heights = jax.random.uniform(jax.random.fold_in(jax.random.fold_in(stream_key, 6), axis_at), (shards_of,), jnp.float32, low / len(pieces), high / len(pieces))
        loudness = loudness * jnp.repeat(jnp.exp(heights), extent[axis_at] // shards_of).reshape((-1,) + (1,) * (len(extent) - 1 - axis_at))
    return loudness


def scatter_about(key, shape, deviation, reach, cuts=(), kind=jnp.bfloat16):
    entries = jax.random.normal(key, shape, jnp.float32) * deviation
    if len(cuts) > 0:
        entries = level_of(key, shape, cuts, -0.22, 0.18) * entries
    return jnp.clip(entries, min=-reach, max=reach).astype(kind)


def setup_inputs(seed: int = 0) -> dict:
    key_list = jax.random.split(jax.random.key(seed), 10)
    obs_coef = scatter_about(key_list[0], (BLOCK, OBS), 0.125, 0.75, ((0, 4), (1, 8)), jnp.float32)
    obs_data = scatter_about(key_list[1], (DATES, OBS), 1.0, 6.0, ((0, 4), (1, 8)), jnp.float32)
    obs_target = draw_obs_target(jax.random.fold_in(key_list[9], 71), 0)
    leaf_map = draw_leaf_map(jax.random.fold_in(key_list[9], 71), 0)
    leaf_parent = with_ends(jax.random.randint(key_list[4], (NLEAF,), 0, NTOP), jax.random.fold_in(key_list[4], 1), 0, NTOP - 1).astype(jnp.int32)
    leaf_inv = draw_leaf_inv(jax.random.fold_in(key_list[9], 71), 0)
    leaf_off = scatter_about(key_list[6], (NLEAF, BLOCK, BLOCK), (BLOCK * NLEAF // NTOP) ** -0.5, 0.25, ((0, 8),), jnp.float32)
    top_inv = draw_top_inv(jax.random.fold_in(key_list[9], 71), 0)
    top_rhs = scatter_about(key_list[8], (NTOP, DATES, BLOCK), 1.0, 6.0, ((1, 4),), jnp.float32)
    return {"obs_coef": obs_coef, "obs_data": obs_data, "obs_target": obs_target, "leaf_map": leaf_map, "leaf_parent": leaf_parent, "leaf_inv": leaf_inv, "leaf_off": leaf_off, "top_inv": top_inv, "top_rhs": top_rhs}


def reference(obs_coef, obs_data, obs_target, leaf_map, leaf_parent, leaf_inv, leaf_off, top_inv, top_rhs):
    highest = lax.Precision.HIGHEST
    position = leaf_map[obs_target].astype(jnp.int32)
    owner_dev = (position // LEAF_DEV).astype(jnp.int32)
    member = (position % LEAF_DEV).astype(jnp.int32)
    row_order = jnp.argsort(owner_dev, stable=True).astype(jnp.int32)
    most_rows = N_LEAF * CAP
    counts = jnp.sum((owner_dev[None, :] == jnp.arange(N_LEAF, dtype=jnp.int32)[:, None]).astype(jnp.int32), axis=1).astype(jnp.int32)
    starts = (jnp.cumsum(counts) - counts).astype(jnp.int32)
    pad_data = jnp.concatenate([obs_data[:, row_order], jnp.zeros((DATES, most_rows), obs_data.dtype)], axis=1)
    pad_coef = jnp.concatenate([obs_coef[:, row_order], jnp.zeros((BLOCK, most_rows), obs_coef.dtype)], axis=1)
    pad_member = jnp.concatenate([member[row_order], jnp.full((most_rows,), -1, jnp.int32)])

    def assemble(device):
        start = starts[device]
        data_rows = lax.dynamic_slice_in_dim(pad_data, start, most_rows, 1)
        coef_rows = lax.dynamic_slice_in_dim(pad_coef, start, most_rows, 1)
        slot_rows = lax.dynamic_slice_in_dim(pad_member, start, most_rows, 0)
        live_rows = jnp.arange(most_rows, dtype=jnp.int32) < counts[device]
        chosen = (slot_rows[None, :] == jnp.arange(LEAF_DEV, dtype=jnp.int32)[:, None]) & live_rows[None, :]
        spread = data_rows[None, :, :] * chosen[:, None, :].astype(data_rows.dtype)
        return jnp.einsum('ltr,cr->ltc', spread, coef_rows, precision=highest)

    leaf_rhs = lax.map(assemble, jnp.arange(N_LEAF, dtype=jnp.int32)).reshape(NLEAF, DATES, BLOCK)
    leaf_y = jnp.einsum('ktc,kdc->ktd', leaf_rhs, leaf_inv, precision=highest)
    holder = jnp.argsort(leaf_map).astype(jnp.int32)
    parent_pos = leaf_parent[holder].astype(jnp.int32)
    update = jnp.einsum('ktd,kcd->ktc', leaf_y, leaf_off, precision=highest)
    top_sum = jax.ops.segment_sum(update, parent_pos, num_segments=NTOP)
    top_y = jnp.einsum('ptc,pdc->ptd', top_rhs - top_sum, top_inv, precision=highest)
    top_solution = jnp.einsum('ptd,pdc->ptc', top_y, top_inv, precision=highest)
    from_top = top_solution[parent_pos]
    lifted = jnp.einsum('ktc,kcd->ktd', from_top, leaf_off, precision=highest)
    leaf_solution = jnp.einsum('ktc,kcd->ktd', leaf_y - lifted, leaf_inv, precision=highest)
    return leaf_solution, top_solution
```

```python
import functools

import jax
import jax.numpy as jnp
from jax import lax
from jax.experimental import pallas as pl
from jax.experimental.pallas import tpu as pltpu
from jax.sharding import PartitionSpec as P

F32, BF16 = jnp.float32, jnp.bfloat16
MESH = pl.DeviceIdType.MESH
LANES = 128


def split(x):
    high = x.astype(BF16)
    return high, (x - high.astype(F32)).astype(BF16)


def contract(a, b, ca, cb):
    return lax.dot_general(a, b, (((ca,), (cb,)), ((), ())), preferred_element_type=F32)


def dot3(a, b, ca, cb):
    (ah, al), (bh, bl) = a, b
    return contract(ah, bh, ca, cb) + (contract(ah, bl, ca, cb) + contract(al, bh, ca, cb))


def kernel(
    groups, shards, capacity,
    tgt, coef, data, lmap, lpar, inv, off, tinv, trhs,
    leaf_out, top_out,
    send, recv, packed, wide, base, parts, arrived, tinv_v, trhs_v,
    d_send, d_recv, f_send, f_recv, r_send, r_recv, g_send, g_recv, l_sem,
):
    me = lax.axis_index("leaf")
    shard = lax.axis_index("rhs")
    local, width = inv.shape[0], inv.shape[1]
    coef_rows, rows = coef.shape
    dates = data.shape[0]
    top_each = tinv_v.shape[0]
    total = lmap.shape[0]
    fold = LANES // coef_rows
    piece = capacity // fold
    pair = f_send.shape[1]
    per = groups // pair
    leaf_peers = [lax.rem(me + o, groups) for o in range(groups)]
    rhs_peers = [lax.rem(shard + o, shards) for o in range(shards)]

    barrier = pltpu.get_barrier_semaphore()
    for o in range(1, groups):
        pl.semaphore_signal(barrier, inc=1, device_id=(leaf_peers[o], shard), device_id_type=MESH)
    for o in range(1, shards):
        pl.semaphore_signal(barrier, inc=1, device_id=(me, rhs_peers[o]), device_id_type=MESH)
    tops = pl.ds(me * top_each, top_each)
    load_inv = pltpu.make_async_copy(tinv.at[tops], tinv_v, l_sem.at[0])
    load_rhs = pltpu.make_async_copy(trhs.at[tops], trhs_v, l_sem.at[1])
    load_inv.start()
    load_rhs.start()

    target = tgt[...]
    position = jnp.zeros_like(target)
    for i in range(total):
        position = jnp.where(target == i, lmap[i], position)
    first = lax.broadcasted_iota(jnp.int32, (groups, rows), 0) * local
    member = jnp.broadcast_to(position, (groups, rows)) - first
    owned = (member >= 0) & (member < local)
    hot = jnp.where(owned, 1.0, 0.0)
    before = (
        lax.broadcasted_iota(jnp.int32, (rows, rows), 0)
        < lax.broadcasted_iota(jnp.int32, (rows, rows), 1)
    )
    rank = contract(hot.astype(BF16), jnp.where(before, 1.0, 0.0).astype(BF16), 1, 0)
    slot = jnp.where(owned, rank.astype(jnp.int32), -1)
    mark = jnp.sum(hot * (member + 1).astype(F32), axis=0, keepdims=True)
    slot_ids = lax.broadcasted_iota(jnp.int32, (capacity, rows), 0)
    chosen = jnp.concatenate(
        [jnp.where(slot_ids == slot[d : d + 1, :], 1.0, 0.0) for d in range(groups)], axis=0
    ).astype(BF16)
    fields = jnp.concatenate(
        [
            coef[...],
            data[...],
            jnp.broadcast_to(mark, (LANES - coef_rows - dates, rows)),
        ],
        axis=0,
    )
    high, low = split(fields)
    payload = contract(chosen, high, 1, 1) + contract(chosen, low, 1, 1)
    send[...] = payload.reshape(groups, capacity, LANES)

    pl.semaphore_wait(barrier, groups - 1 + shards - 1)
    row_copies = []
    for o in range(1, groups):
        copy = pltpu.make_async_remote_copy(
            src_ref=send.at[leaf_peers[o]],
            dst_ref=recv.at[o],
            send_sem=d_send.at[o],
            recv_sem=d_recv.at[o],
            device_id=(leaf_peers[o], shard),
            device_id_type=MESH,
        )
        copy.start()
        row_copies.append(copy)
    recv[0] = send[me]

    for l in range(local):
        high, low = split(dot3(split(off[l]), split(inv[l]), 1, 0))
        wide[0, l] = high
        wide[1, l] = low
    load_inv.wait()
    load_rhs.wait()
    gram = []
    for i in range(top_each):
        block = split(tinv_v[i])
        gram.append(split(dot3(block, block, 0, 0)))
    up = []
    for l in range(local):
        found = jnp.int32(0)
        for i in range(total):
            found = jnp.where(lmap[i] == me * local + l, lpar[i], found)
        up.append(found)

    lane_group = lax.broadcasted_iota(jnp.int32, (piece, LANES), 1) // coef_rows
    forwards = []
    for g in range(pair):
        for o in range(g * per, (g + 1) * per):
            if o > 0:
                row_copies[o - 1].wait_recv()
            block = recv[o]
            out = block[:piece]
            for q in range(1, fold):
                moved = pltpu.roll(block[q * piece : (q + 1) * piece], q * coef_rows, 1)
                out = jnp.where(lane_group == q, moved, out)
            packed[shard, o] = out
        span = pl.ds(g * per, per)
        for o in range(1, shards):
            copy = pltpu.make_async_remote_copy(
                src_ref=packed.at[shard, span],
                dst_ref=packed.at[shard, span],
                send_sem=f_send.at[o, g],
                recv_sem=f_recv.at[o, g],
                device_id=(me, rhs_peers[o]),
                device_id_type=MESH,
            )
            copy.start()
            forwards.append(copy)
    slots = groups * capacity
    rows_in = recv[...].reshape(slots, LANES)
    turned = split(rows_in.T)
    marks = rows_in[:, coef_rows + dates : coef_rows + dates + 1]
    for copy in forwards:
        copy.wait_recv()

    packs = [packed[s].reshape(groups * piece, LANES) for s in range(shards)]
    big_group = lax.broadcasted_iota(jnp.int32, (groups * piece, LANES), 1) // coef_rows
    pieces = []
    for q in range(fold):
        out = None
        for s in range(shards):
            shift = ((s - q) * coef_rows) % LANES
            moved = pltpu.roll(packs[s], shift, 1) if shift else packs[s]
            out = moved if out is None else jnp.where(big_group == s, moved, out)
        pieces.append(out.reshape(groups, 1, piece, LANES))
    coefs = jnp.concatenate(pieces, axis=1).reshape(slots, LANES)
    spread = jnp.concatenate(
        [jnp.where(marks == float(l + 1), coefs, 0.0) for l in range(local)], axis=1
    )
    rhs_all = dot3(turned, split(spread), 1, 0)[coef_rows : coef_rows + dates]
    rhs = [split(rhs_all[:, l * width : (l + 1) * width]) for l in range(local)]
    updates = [dot3(rhs[l], (wide[0, l], wide[1, l]), 1, 1) for l in range(local)]
    tops_all = top_out.shape[0]
    for p in range(tops_all):
        acc = None
        for l in range(local):
            term = jnp.where(up[l] == p, 1.0, 0.0) * updates[l]
            acc = term if acc is None else acc + term
        parts[p] = acc
    sums = []
    for o in range(1, groups):
        copy = pltpu.make_async_remote_copy(
            src_ref=parts.at[pl.ds(leaf_peers[o] * top_each, top_each)],
            dst_ref=arrived.at[o],
            send_sem=r_send.at[o],
            recv_sem=r_recv.at[o],
            device_id=(leaf_peers[o], shard),
            device_id_type=MESH,
        )
        copy.start()
        sums.append(copy)
    for l in range(local):
        factor = split(inv[l])
        solved = split(dot3(rhs[l], factor, 1, 1))
        base[l] = dot3(solved, factor, 1, 0)
    residue = [trhs_v[i] - parts[me * top_each + i] for i in range(top_each)]
    for o in range(1, groups):
        sums[o - 1].wait_recv()
        residue = [residue[i] - arrived[o, i] for i in range(top_each)]
    for i in range(top_each):
        top_out[me * top_each + i] = dot3(split(residue[i]), gram[i], 1, 0)
    solutions = []
    for o in range(1, groups):
        copy = pltpu.make_async_remote_copy(
            src_ref=top_out.at[tops],
            dst_ref=top_out.at[tops],
            send_sem=g_send.at[o],
            recv_sem=g_recv.at[o],
            device_id=(leaf_peers[o], shard),
            device_id_type=MESH,
        )
        copy.start()
        solutions.append(copy)
    for copy in row_copies + forwards + sums:
        copy.wait_send()
    for copy in solutions:
        copy.wait_recv()
    for l in range(local):
        lifted = dot3(split(top_out[up[l]]), (wide[0, l], wide[1, l]), 1, 0)
        leaf_out[l] = base[l] - lifted
    for copy in solutions:
        copy.wait_send()


def fused(
    obs_coef, obs_data, obs_target, leaf_map, leaf_parent, leaf_inv, leaf_off, top_inv, top_rhs
):
    groups, shards = lax.axis_size("leaf"), lax.axis_size("rhs")
    rows = obs_target.shape[0]
    capacity = 2 * rows // groups
    local, width = leaf_inv.shape[0], leaf_inv.shape[1]
    top_count, dates = top_inv.shape[0], obs_data.shape[0]
    top_each = top_count // groups
    coef_rows = obs_coef.shape[0]
    piece = capacity * coef_rows // LANES
    pair = groups // 2 if groups % 2 == 0 else groups
    dma = pltpu.SemaphoreType.DMA
    vmem = pl.BlockSpec(memory_space=pltpu.VMEM)
    smem = pl.BlockSpec(memory_space=pltpu.SMEM)
    hbm = pl.BlockSpec(memory_space=pl.ANY)
    return pl.pallas_call(
        functools.partial(kernel, groups, shards, capacity),
        out_shape=(
            jax.ShapeDtypeStruct((local, dates, width), F32),
            jax.ShapeDtypeStruct((top_count, dates, width), F32),
        ),
        in_specs=[vmem, vmem, vmem, smem, smem, vmem, vmem, hbm, hbm],
        out_specs=(vmem, vmem),
        scratch_shapes=[
            pltpu.VMEM((groups, capacity, LANES), F32),
            pltpu.VMEM((groups, capacity, LANES), F32),
            pltpu.VMEM((shards, groups, piece, LANES), F32),
            pltpu.VMEM((2, local, width, width), BF16),
            pltpu.VMEM((local, dates, width), F32),
            pltpu.VMEM((top_count, dates, width), F32),
            pltpu.VMEM((groups, top_each, dates, width), F32),
            pltpu.VMEM((top_each, width, width), F32),
            pltpu.VMEM((top_each, dates, width), F32),
            dma((groups,)),
            dma((groups,)),
            dma((shards, pair)),
            dma((shards, pair)),
            dma((groups,)),
            dma((groups,)),
            dma((groups,)),
            dma((groups,)),
            dma((2,)),
        ],
        compiler_params=pltpu.CompilerParams(
            collective_id=0, has_side_effects=True, vmem_limit_bytes=24 * 2**20
        ),
    )(
        obs_target.reshape(1, rows), obs_coef, obs_data, leaf_map, leaf_parent,
        leaf_inv, leaf_off, top_inv, top_rhs,
    )


def plain(
    obs_coef, obs_data, obs_target, leaf_map, leaf_parent, leaf_inv, leaf_off, top_inv, top_rhs
):
    highest = lax.Precision.HIGHEST
    groups = lax.axis_size("leaf")
    device_index = lax.axis_index("leaf")
    local_count = leaf_inv.shape[0]
    block_width = leaf_inv.shape[1]
    top_count = top_inv.shape[0]
    date_cols = obs_data.shape[0]
    rows_here = obs_target.shape[0]
    leaf_total = leaf_map.shape[0]
    capacity = max(2, 2 * rows_here // groups)
    slots_total = groups * capacity
    all_ids = jnp.arange(leaf_total, dtype=jnp.int32)
    id_match = obs_target[:, None] == all_ids[None, :]
    position = jnp.sum(jnp.where(id_match, leaf_map[None, :], 0), axis=1)
    owner_dev = position // local_count
    member = position % local_count
    row_ids = jnp.arange(rows_here, dtype=jnp.int32)
    earlier = (owner_dev[:, None] == owner_dev[None, :]) & (row_ids[:, None] > row_ids[None, :])
    queue_rank = jnp.sum(earlier.astype(jnp.int32), axis=1)
    target_slot = owner_dev * capacity + queue_rank
    slot_mark = (member + 1).astype(jnp.float32)[None, :]
    fields = jnp.concatenate([obs_coef, obs_data, slot_mark], axis=0)
    placed = jnp.zeros((fields.shape[0], slots_total), F32).at[:, target_slot].set(fields)
    received = lax.all_to_all(placed, "leaf", split_axis=1, concat_axis=1, tiled=True)
    part_coef = received[: obs_coef.shape[0]]
    recv_data = received[obs_coef.shape[0] : -1]
    recv_mark = received[-1:]
    recv_coef = lax.all_gather(part_coef, "rhs", axis=0, tiled=True)
    slot_values = (jnp.arange(local_count, dtype=jnp.int32) + 1).astype(jnp.float32)
    chosen = (recv_mark[0][None, :] == slot_values[:, None]).astype(jnp.float32)
    spread = (recv_data[None, :, :] * chosen[:, None, :]).reshape(
        local_count * date_cols, slots_total
    )
    leaf_rhs = lax.dot_general(
        spread, recv_coef, (((1,), (1,)), ((), ())), precision=highest
    ).reshape(local_count, date_cols, block_width)
    solved = jnp.einsum("ltc,ldc->ltd", leaf_rhs, leaf_inv, precision=highest)
    update = jnp.einsum("ltd,lcd->ltc", solved, leaf_off, precision=highest)
    positions_here = device_index * local_count + jnp.arange(local_count, dtype=jnp.int32)
    holder_match = leaf_map[None, :] == positions_here[:, None]
    parent_here = jnp.sum(jnp.where(holder_match, leaf_parent[None, :], 0), axis=1)
    to_top = (parent_here[:, None] == jnp.arange(top_count, dtype=jnp.int32)[None, :]).astype(
        jnp.float32
    )
    contrib = jnp.einsum("lp,ltc->ptc", to_top, update, precision=highest)
    flat_terms = contrib.reshape(top_count * date_cols, block_width)
    top_total = lax.psum(flat_terms, "leaf").reshape(top_count, date_cols, block_width)
    residue = top_rhs - top_total
    top_solved = jnp.einsum("ptc,pdc->ptd", residue, top_inv, precision=highest)
    top_solution = jnp.einsum("ptd,pdc->ptc", top_solved, top_inv, precision=highest)
    from_top = jnp.einsum("lp,ptc->ltc", to_top, top_solution, precision=highest)
    lifted = jnp.einsum("ltc,lcd->ltd", from_top, leaf_off, precision=highest)
    leaf_solution = jnp.einsum("ltc,lcd->ltd", solved - lifted, leaf_inv, precision=highest)
    return (leaf_solution, top_solution)


def body(*args):
    obs_coef, obs_data, obs_target = args[:3]
    groups = lax.axis_size("leaf")
    coef_rows, rows = obs_coef.shape
    dates = obs_data.shape[0]
    fits = (
        args[7].shape[0] % groups == 0
        and rows % LANES == 0
        and (2 * rows) % groups == 0
        and LANES % coef_rows == 0
        and (2 * rows // groups) % (8 * (LANES // coef_rows)) == 0
        and coef_rows % 8 == 0
        and dates % 8 == 0
        and coef_rows + dates < LANES
        and args[5].shape[1] == LANES
    )
    return fused(*args) if fits else plain(*args)


def solution(mesh):
    return jax.shard_map(
        body,
        mesh=mesh,
        in_specs=(
            P("rhs", "leaf"),
            P("rhs", "leaf"),
            P("leaf"),
            P(),
            P(),
            P("leaf", None, None),
            P("leaf", None, None),
            P(),
            P(None, "rhs", None),
        ),
        out_specs=(P("leaf", "rhs", None), P(None, "rhs", None)),
        check_vma=False,
    )
```

```python
import functools

import jax
import jax.numpy as jnp
from jax import lax
from jax.experimental import pallas as pl
from jax.experimental.pallas import tpu as pltpu
from jax.sharding import PartitionSpec as P

F32, BF16 = jnp.float32, jnp.bfloat16
MESH = pl.DeviceIdType.MESH
LANES = 128


def split(x):
    high = x.astype(BF16)
    return high, (x - high.astype(F32)).astype(BF16)


def contract(a, b, ca, cb):
    return lax.dot_general(a, b, (((ca,), (cb,)), ((), ())), preferred_element_type=F32)


def dot3(a, b, ca, cb):
    (ah, al), (bh, bl) = a, b
    return contract(ah, bh, ca, cb) + (contract(ah, bl, ca, cb) + contract(al, bh, ca, cb))


def flipped(index, bits, count):
    out = index
    place = 1
    while place < count:
        if bits & place:
            out = out + place * (1 - 2 * lax.rem(lax.div(index, place), 2))
        place *= 2
    return out


def kernel(
    groups, shards, capacity,
    tgt_h, coef_h, data_h, lmap_h, lpar_h, inv_h, off_h, tinv_h, trhs_h,
    leaf_out, top_out,
    tgt, coef, data, lmap, lpar, inv, off, tinv, trhs,
    send, recv, packed, wide, base, parts, across, joined, along,
    d_send, d_recv, f_send, f_recv, a_send, a_recv, z_send, z_recv, g_send, g_recv, l_sem,
):
    me = lax.axis_index("leaf")
    shard = lax.axis_index("rhs")
    local, width = inv.shape[0], inv.shape[1]
    coef_rows, rows = coef.shape
    dates = data.shape[0]
    top_each = tinv.shape[0]
    total = lmap.shape[0]
    fold = LANES // coef_rows
    piece = capacity // fold
    pair = f_send.shape[1]
    per = groups // pair
    leaf_peers = [flipped(me, o, groups) for o in range(groups)]
    far_first = sorted(range(1, groups), key=lambda o: (-(o.bit_length()), o))
    rhs_peers = [lax.rem(shard + o, shards) for o in range(shards)]

    barrier = pltpu.get_barrier_semaphore()
    for o in range(1, groups):
        pl.semaphore_signal(barrier, inc=1, device_id=(leaf_peers[o], shard), device_id_type=MESH)
    for o in range(1, shards):
        pl.semaphore_signal(barrier, inc=1, device_id=(me, rhs_peers[o]), device_id_type=MESH)
    tops = pl.ds(me * top_each, top_each)
    loads = []
    for i, (src, dst) in enumerate(
        [
            (tgt_h, tgt),
            (lmap_h, lmap),
            (coef_h, coef),
            (data_h, data),
            (lpar_h, lpar),
            (inv_h, inv),
            (off_h, off),
            (tinv_h.at[tops], tinv),
            (trhs_h.at[tops], trhs),
        ]
    ):
        copy = pltpu.make_async_copy(src, dst, l_sem.at[i])
        copy.start()
        loads.append(copy)
    loads[0].wait()
    loads[1].wait()

    target = tgt[...]
    position = jnp.zeros_like(target)
    for i in range(total):
        position = jnp.where(target == i, lmap[i], position)
    first = lax.broadcasted_iota(jnp.int32, (groups, rows), 0) * local
    member = jnp.broadcast_to(position, (groups, rows)) - first
    owned = (member >= 0) & (member < local)
    hot = jnp.where(owned, 1.0, 0.0)
    before = (
        lax.broadcasted_iota(jnp.int32, (rows, rows), 0)
        < lax.broadcasted_iota(jnp.int32, (rows, rows), 1)
    )
    rank = contract(hot.astype(BF16), jnp.where(before, 1.0, 0.0).astype(BF16), 1, 0)
    slot = jnp.where(owned, rank.astype(jnp.int32), -1)
    mark = jnp.sum(hot * (member + 1).astype(F32), axis=0, keepdims=True)
    slot_ids = lax.broadcasted_iota(jnp.int32, (capacity, rows), 0)
    chosen = jnp.concatenate(
        [jnp.where(slot_ids == slot[d : d + 1, :], 1.0, 0.0) for d in range(groups)], axis=0
    ).astype(BF16)
    loads[2].wait()
    loads[3].wait()
    fields = jnp.concatenate(
        [
            coef[...],
            data[...],
            jnp.broadcast_to(mark, (LANES - coef_rows - dates, rows)),
        ],
        axis=0,
    )
    high, low = split(fields)
    payload = contract(chosen, high, 1, 1) + contract(chosen, low, 1, 1)
    send[...] = payload.reshape(groups, capacity, LANES)

    pl.semaphore_wait(barrier, groups - 1 + shards - 1)
    row_copies = {}
    for o in far_first:
        copy = pltpu.make_async_remote_copy(
            src_ref=send.at[leaf_peers[o]],
            dst_ref=recv.at[o],
            send_sem=d_send.at[o],
            recv_sem=d_recv.at[o],
            device_id=(leaf_peers[o], shard),
            device_id_type=MESH,
        )
        copy.start()
        row_copies[o] = copy
    recv[0] = send[me]

    for copy in loads[4:]:
        copy.wait()
    for l in range(local):
        high, low = split(dot3(split(off[l]), split(inv[l]), 1, 0))
        wide[0, l] = high
        wide[1, l] = low
    gram = []
    for i in range(top_each):
        block = split(tinv[i])
        gram.append(split(dot3(block, block, 0, 0)))
    up = []
    for l in range(local):
        found = jnp.int32(0)
        for i in range(total):
            found = jnp.where(lmap[i] == me * local + l, lpar[i], found)
        up.append(found)

    lane_group = lax.broadcasted_iota(jnp.int32, (piece, LANES), 1) // coef_rows
    forwards = []
    for g in range(pair):
        for o in range(g * per, (g + 1) * per):
            if o > 0:
                row_copies[o].wait_recv()
            block = recv[o]
            out = block[:piece]
            for q in range(1, fold):
                moved = pltpu.roll(block[q * piece : (q + 1) * piece], q * coef_rows, 1)
                out = jnp.where(lane_group == q, moved, out)
            packed[shard, o] = out
        span = pl.ds(g * per, per)
        for o in range(1, shards):
            copy = pltpu.make_async_remote_copy(
                src_ref=packed.at[shard, span],
                dst_ref=packed.at[shard, span],
                send_sem=f_send.at[o, g],
                recv_sem=f_recv.at[o, g],
                device_id=(me, rhs_peers[o]),
                device_id_type=MESH,
            )
            copy.start()
            forwards.append(copy)
    slots = groups * capacity
    rows_in = recv[...].reshape(slots, LANES)
    turned = split(rows_in.T)
    marks = rows_in[:, coef_rows + dates : coef_rows + dates + 1]
    for copy in forwards:
        copy.wait_recv()

    packs = [packed[s].reshape(groups * piece, LANES) for s in range(shards)]
    big_group = lax.broadcasted_iota(jnp.int32, (groups * piece, LANES), 1) // coef_rows
    pieces = []
    for q in range(fold):
        out = None
        for s in range(shards):
            shift = ((s - q) * coef_rows) % LANES
            moved = pltpu.roll(packs[s], shift, 1) if shift else packs[s]
            out = moved if out is None else jnp.where(big_group == s, moved, out)
        pieces.append(out.reshape(groups, 1, piece, LANES))
    coefs = jnp.concatenate(pieces, axis=1).reshape(slots, LANES)
    spread = jnp.concatenate(
        [jnp.where(marks == float(l + 1), coefs, 0.0) for l in range(local)], axis=1
    )
    rhs_all = dot3(turned, split(spread), 1, 0)[coef_rows : coef_rows + dates]
    rhs = [split(rhs_all[:, l * width : (l + 1) * width]) for l in range(local)]
    updates = [dot3(rhs[l], (wide[0, l], wide[1, l]), 1, 1) for l in range(local)]
    tops_all = top_out.shape[0]
    for p in range(tops_all):
        acc = None
        for l in range(local):
            term = jnp.where(up[l] == p, 1.0, 0.0) * updates[l]
            acc = term if acc is None else acc + term
        parts[p] = acc
    steps = [h // 2 for h in far_first if h % 2 == 0] + [0]
    cross = {}
    for h in steps:
        copy = pltpu.make_async_remote_copy(
            src_ref=parts.at[pl.ds(leaf_peers[2 * h + 1] * top_each, top_each)],
            dst_ref=across.at[h],
            send_sem=a_send.at[h],
            recv_sem=a_recv.at[h],
            device_id=(leaf_peers[1], shard),
            device_id_type=MESH,
        )
        copy.start()
        cross[h] = copy
    sums = {}
    for h in steps:
        cross[h].wait_recv()
        here = parts[pl.ds(leaf_peers[2 * h] * top_each, top_each)] + across[h]
        if h == 0:
            residue = trhs[...] - here
            continue
        joined[h] = here
        copy = pltpu.make_async_remote_copy(
            src_ref=joined.at[h],
            dst_ref=along.at[h],
            send_sem=z_send.at[h],
            recv_sem=z_recv.at[h],
            device_id=(leaf_peers[2 * h], shard),
            device_id_type=MESH,
        )
        copy.start()
        sums[h] = copy
    for l in range(local):
        factor = split(inv[l])
        solved = split(dot3(rhs[l], factor, 1, 1))
        base[l] = dot3(solved, factor, 1, 0)
    for h in steps[:-1]:
        sums[h].wait_recv()
        residue = residue - along[h]
    for i in range(top_each):
        top_out[me * top_each + i] = dot3(split(residue[i]), gram[i], 1, 0)
    solutions = {}
    for o in steps[:-1]:
        copy = pltpu.make_async_remote_copy(
            src_ref=top_out.at[tops],
            dst_ref=top_out.at[tops],
            send_sem=g_send.at[2 * o],
            recv_sem=g_recv.at[2 * o],
            device_id=(leaf_peers[2 * o], shard),
            device_id_type=MESH,
        )
        copy.start()
        solutions[2 * o] = copy
    for h in reversed(steps):
        if h > 0:
            solutions[2 * h].wait_recv()
        block = pl.ds(leaf_peers[2 * h] * top_each, top_each)
        copy = pltpu.make_async_remote_copy(
            src_ref=top_out.at[block],
            dst_ref=top_out.at[block],
            send_sem=g_send.at[2 * h + 1],
            recv_sem=g_recv.at[2 * h + 1],
            device_id=(leaf_peers[1], shard),
            device_id_type=MESH,
        )
        copy.start()
        solutions[2 * h + 1] = copy
    for copy in [*row_copies.values(), *forwards, *cross.values(), *sums.values()]:
        copy.wait_send()
    for h in reversed(steps):
        solutions[2 * h + 1].wait_recv()
    for l in range(local):
        lifted = dot3(split(top_out[up[l]]), (wide[0, l], wide[1, l]), 1, 0)
        leaf_out[l] = base[l] - lifted
    for copy in solutions.values():
        copy.wait_send()


def fused(
    obs_coef, obs_data, obs_target, leaf_map, leaf_parent, leaf_inv, leaf_off, top_inv, top_rhs
):
    groups, shards = lax.axis_size("leaf"), lax.axis_size("rhs")
    rows = obs_target.shape[0]
    capacity = 2 * rows // groups
    local, width = leaf_inv.shape[0], leaf_inv.shape[1]
    top_count, dates = top_inv.shape[0], obs_data.shape[0]
    top_each = top_count // groups
    coef_rows = obs_coef.shape[0]
    piece = capacity * coef_rows // LANES
    pair = groups // 2
    dma = pltpu.SemaphoreType.DMA
    vmem = pl.BlockSpec(memory_space=pltpu.VMEM)
    hbm = pl.BlockSpec(memory_space=pl.ANY)
    return pl.pallas_call(
        functools.partial(kernel, groups, shards, capacity),
        out_shape=(
            jax.ShapeDtypeStruct((local, dates, width), F32),
            jax.ShapeDtypeStruct((top_count, dates, width), F32),
        ),
        in_specs=[hbm] * 9,
        out_specs=(vmem, vmem),
        scratch_shapes=[
            pltpu.VMEM((1, rows), jnp.int32),
            pltpu.VMEM(obs_coef.shape, F32),
            pltpu.VMEM(obs_data.shape, F32),
            pltpu.SMEM(leaf_map.shape, jnp.int32),
            pltpu.SMEM(leaf_parent.shape, jnp.int32),
            pltpu.VMEM(leaf_inv.shape, F32),
            pltpu.VMEM(leaf_off.shape, F32),
            pltpu.VMEM((top_each, width, width), F32),
            pltpu.VMEM((top_each, dates, width), F32),
            pltpu.VMEM((groups, capacity, LANES), F32),
            pltpu.VMEM((groups, capacity, LANES), F32),
            pltpu.VMEM((shards, groups, piece, LANES), F32),
            pltpu.VMEM((2, local, width, width), BF16),
            pltpu.VMEM((local, dates, width), F32),
            pltpu.VMEM((top_count, dates, width), F32),
            pltpu.VMEM((groups // 2, top_each, dates, width), F32),
            pltpu.VMEM((groups // 2, top_each, dates, width), F32),
            pltpu.VMEM((groups // 2, top_each, dates, width), F32),
            dma((groups,)),
            dma((groups,)),
            dma((shards, pair)),
            dma((shards, pair)),
            dma((groups // 2,)),
            dma((groups // 2,)),
            dma((groups // 2,)),
            dma((groups // 2,)),
            dma((groups,)),
            dma((groups,)),
            dma((9,)),
        ],
        compiler_params=pltpu.CompilerParams(
            collective_id=0, has_side_effects=True, vmem_limit_bytes=60 * 2**20
        ),
    )(
        obs_target.reshape(1, rows), obs_coef, obs_data, leaf_map, leaf_parent,
        leaf_inv, leaf_off, top_inv, top_rhs,
    )


def plain(
    obs_coef, obs_data, obs_target, leaf_map, leaf_parent, leaf_inv, leaf_off, top_inv, top_rhs
):
    highest = lax.Precision.HIGHEST
    groups = lax.axis_size("leaf")
    device_index = lax.axis_index("leaf")
    local_count = leaf_inv.shape[0]
    block_width = leaf_inv.shape[1]
    top_count = top_inv.shape[0]
    date_cols = obs_data.shape[0]
    rows_here = obs_target.shape[0]
    leaf_total = leaf_map.shape[0]
    capacity = max(2, 2 * rows_here // groups)
    slots_total = groups * capacity
    all_ids = jnp.arange(leaf_total, dtype=jnp.int32)
    id_match = obs_target[:, None] == all_ids[None, :]
    position = jnp.sum(jnp.where(id_match, leaf_map[None, :], 0), axis=1)
    owner_dev = position // local_count
    member = position % local_count
    row_ids = jnp.arange(rows_here, dtype=jnp.int32)
    earlier = (owner_dev[:, None] == owner_dev[None, :]) & (row_ids[:, None] > row_ids[None, :])
    queue_rank = jnp.sum(earlier.astype(jnp.int32), axis=1)
    target_slot = owner_dev * capacity + queue_rank
    slot_mark = (member + 1).astype(jnp.float32)[None, :]
    fields = jnp.concatenate([obs_coef, obs_data, slot_mark], axis=0)
    placed = jnp.zeros((fields.shape[0], slots_total), F32).at[:, target_slot].set(fields)
    received = lax.all_to_all(placed, "leaf", split_axis=1, concat_axis=1, tiled=True)
    part_coef = received[: obs_coef.shape[0]]
    recv_data = received[obs_coef.shape[0] : -1]
    recv_mark = received[-1:]
    recv_coef = lax.all_gather(part_coef, "rhs", axis=0, tiled=True)
    slot_values = (jnp.arange(local_count, dtype=jnp.int32) + 1).astype(jnp.float32)
    chosen = (recv_mark[0][None, :] == slot_values[:, None]).astype(jnp.float32)
    spread = (recv_data[None, :, :] * chosen[:, None, :]).reshape(
        local_count * date_cols, slots_total
    )
    leaf_rhs = lax.dot_general(
        spread, recv_coef, (((1,), (1,)), ((), ())), precision=highest
    ).reshape(local_count, date_cols, block_width)
    solved = jnp.einsum("ltc,ldc->ltd", leaf_rhs, leaf_inv, precision=highest)
    update = jnp.einsum("ltd,lcd->ltc", solved, leaf_off, precision=highest)
    positions_here = device_index * local_count + jnp.arange(local_count, dtype=jnp.int32)
    holder_match = leaf_map[None, :] == positions_here[:, None]
    parent_here = jnp.sum(jnp.where(holder_match, leaf_parent[None, :], 0), axis=1)
    to_top = (parent_here[:, None] == jnp.arange(top_count, dtype=jnp.int32)[None, :]).astype(
        jnp.float32
    )
    contrib = jnp.einsum("lp,ltc->ptc", to_top, update, precision=highest)
    flat_terms = contrib.reshape(top_count * date_cols, block_width)
    top_total = lax.psum(flat_terms, "leaf").reshape(top_count, date_cols, block_width)
    residue = top_rhs - top_total
    top_solved = jnp.einsum("ptc,pdc->ptd", residue, top_inv, precision=highest)
    top_solution = jnp.einsum("ptd,pdc->ptc", top_solved, top_inv, precision=highest)
    from_top = jnp.einsum("lp,ptc->ltc", to_top, top_solution, precision=highest)
    lifted = jnp.einsum("ltc,lcd->ltd", from_top, leaf_off, precision=highest)
    leaf_solution = jnp.einsum("ltc,lcd->ltd", solved - lifted, leaf_inv, precision=highest)
    return (leaf_solution, top_solution)


def body(*args):
    obs_coef, obs_data, obs_target = args[:3]
    groups = lax.axis_size("leaf")
    coef_rows, rows = obs_coef.shape
    dates = obs_data.shape[0]
    fits = (
        args[7].shape[0] % groups == 0
        and groups > 1
        and groups & (groups - 1) == 0
        and rows % LANES == 0
        and (2 * rows) % groups == 0
        and LANES % coef_rows == 0
        and (2 * rows // groups) % (8 * (LANES // coef_rows)) == 0
        and coef_rows % 8 == 0
        and dates % 8 == 0
        and coef_rows + dates < LANES
        and args[5].shape[1] == LANES
    )
    return fused(*args) if fits else plain(*args)


def solution(mesh):
    return jax.shard_map(
        body,
        mesh=mesh,
        in_specs=(
            P("rhs", "leaf"),
            P("rhs", "leaf"),
            P("leaf"),
            P(),
            P(),
            P("leaf", None, None),
            P("leaf", None, None),
            P(),
            P(None, "rhs", None),
        ),
        out_specs=(P("leaf", "rhs", None), P(None, "rhs", None)),
        check_vma=False,
    )
```

```python
import functools

import jax
import jax.numpy as jnp
from jax import lax
from jax.experimental import pallas as pl
from jax.experimental.pallas import tpu as pltpu
from jax.sharding import PartitionSpec as P

F32, BF16 = jnp.float32, jnp.bfloat16
MESH = pl.DeviceIdType.MESH
LANES = 128


def split(x):
    high = x.astype(BF16)
    return high, (x - high.astype(F32)).astype(BF16)


def contract(a, b, ca, cb):
    return lax.dot_general(a, b, (((ca,), (cb,)), ((), ())), preferred_element_type=F32)


def dot3(a, b, ca, cb):
    (ah, al), (bh, bl) = a, b
    return contract(ah, bh, ca, cb) + (contract(ah, bl, ca, cb) + contract(al, bh, ca, cb))


def flipped(index, bits, count):
    out = index
    place = 1
    while place < count:
        if bits & place:
            out = out + place * (1 - 2 * lax.rem(lax.div(index, place), 2))
        place *= 2
    return out


def kernel(
    groups, shards, capacity,
    tgt_h, coef_h, data_h, lmap_h, lpar_h, inv_h, off_h, tinv_h, trhs_h,
    leaf_out, top_out,
    tgt, coef, data, lmap, lpar, inv, off, tinv, trhs,
    send, recv, packed, wide, base, parts, across, joined, along,
    d_send, d_recv, f_send, f_recv, a_send, a_recv, z_send, z_recv, g_send, g_recv, l_sem,
):
    me = lax.axis_index("leaf")
    shard = lax.axis_index("rhs")
    local, width = inv.shape[0], inv.shape[1]
    coef_rows, rows = coef.shape
    dates = data.shape[0]
    top_each = tinv.shape[0]
    total = lmap.shape[0]
    fold = LANES // coef_rows
    piece = capacity // fold
    pair = f_send.shape[1]
    cuts, tops_all, half = parts.shape[0], parts.shape[1], parts.shape[2]
    per = groups // pair
    leaf_peers = [flipped(me, o, groups) for o in range(groups)]
    far_first = sorted(range(1, groups), key=lambda o: (-(o.bit_length()), o))
    rhs_peers = [lax.rem(shard + o, shards) for o in range(shards)]

    barrier = pltpu.get_barrier_semaphore()
    for o in range(1, groups):
        pl.semaphore_signal(barrier, inc=1, device_id=(leaf_peers[o], shard), device_id_type=MESH)
    for o in range(1, shards):
        pl.semaphore_signal(barrier, inc=1, device_id=(me, rhs_peers[o]), device_id_type=MESH)
    tops = pl.ds(me * top_each, top_each)
    loads = []
    for i, (src, dst) in enumerate(
        [
            (tgt_h, tgt),
            (lmap_h, lmap),
            (coef_h, coef),
            (data_h, data),
            (lpar_h, lpar),
            (inv_h, inv),
            (off_h, off),
            (tinv_h.at[tops], tinv),
            (trhs_h.at[tops], trhs),
        ]
    ):
        copy = pltpu.make_async_copy(src, dst, l_sem.at[i])
        copy.start()
        loads.append(copy)
    loads[0].wait()
    loads[1].wait()

    target = tgt[...]
    position = jnp.zeros_like(target)
    for i in range(total):
        position = jnp.where(target == i, lmap[i], position)
    place = lax.broadcasted_iota(jnp.int32, (groups, rows), 0)
    first = jnp.zeros_like(place)
    for o in range(groups):
        first = jnp.where(place == o, leaf_peers[o] * local, first)
    member = jnp.broadcast_to(position, (groups, rows)) - first
    owned = (member >= 0) & (member < local)
    hot = jnp.where(owned, 1.0, 0.0)
    before = (
        lax.broadcasted_iota(jnp.int32, (rows, rows), 0)
        < lax.broadcasted_iota(jnp.int32, (rows, rows), 1)
    )
    rank = contract(hot.astype(BF16), jnp.where(before, 1.0, 0.0).astype(BF16), 1, 0)
    slot = jnp.where(owned, rank.astype(jnp.int32), -1)
    mark = jnp.sum(hot * (member + 1).astype(F32), axis=0, keepdims=True)
    slot_ids = lax.broadcasted_iota(jnp.int32, (capacity, rows), 0)
    loads[2].wait()
    loads[3].wait()
    fields = jnp.concatenate(
        [
            coef[...],
            data[...],
            jnp.broadcast_to(mark, (LANES - coef_rows - dates, rows)),
        ],
        axis=0,
    )
    high, low = split(fields)

    def placed(o):
        chosen = jnp.where(slot_ids == slot[o : o + 1, :], 1.0, 0.0).astype(BF16)
        return contract(chosen, high, 1, 1) + contract(chosen, low, 1, 1)

    pl.semaphore_wait(barrier, groups - 1 + shards - 1)
    row_copies = {}
    for o in far_first:
        send[o] = placed(o)
        copy = pltpu.make_async_remote_copy(
            src_ref=send.at[o],
            dst_ref=recv.at[o],
            send_sem=d_send.at[o],
            recv_sem=d_recv.at[o],
            device_id=(leaf_peers[o], shard),
            device_id_type=MESH,
        )
        copy.start()
        row_copies[o] = copy
    recv[0] = placed(0)

    for copy in loads[4:]:
        copy.wait()
    for l in range(local):
        high, low = split(dot3(split(off[l]), split(inv[l]), 1, 0))
        wide[0, l] = high
        wide[1, l] = low
    gram = []
    for i in range(top_each):
        block = split(tinv[i])
        gram.append(split(dot3(block, block, 0, 0)))
    up = []
    for l in range(local):
        found = jnp.int32(0)
        for i in range(total):
            found = jnp.where(lmap[i] == me * local + l, lpar[i], found)
        up.append(found)

    lane_group = lax.broadcasted_iota(jnp.int32, (piece, LANES), 1) // coef_rows
    forwards = []
    for g in range(pair):
        for o in range(g * per, (g + 1) * per):
            if o > 0:
                row_copies[o].wait_recv()
            block = recv[o]
            out = block[:piece]
            for q in range(1, fold):
                moved = pltpu.roll(block[q * piece : (q + 1) * piece], q * coef_rows, 1)
                out = jnp.where(lane_group == q, moved, out)
            packed[shard, o] = out
        span = pl.ds(g * per, per)
        for o in range(1, shards):
            copy = pltpu.make_async_remote_copy(
                src_ref=packed.at[shard, span],
                dst_ref=packed.at[shard, span],
                send_sem=f_send.at[o, g],
                recv_sem=f_recv.at[o, g],
                device_id=(me, rhs_peers[o]),
                device_id_type=MESH,
            )
            copy.start()
            forwards.append(copy)
    slots = groups * capacity
    rows_in = recv[...].reshape(slots, LANES)
    turned = split(rows_in.T)
    marks = rows_in[:, coef_rows + dates : coef_rows + dates + 1]
    for copy in forwards:
        copy.wait_recv()

    packs = [packed[s].reshape(groups * piece, LANES) for s in range(shards)]
    big_group = lax.broadcasted_iota(jnp.int32, (groups * piece, LANES), 1) // coef_rows
    pieces = []
    for q in range(fold):
        out = None
        for s in range(shards):
            shift = ((s - q) * coef_rows) % LANES
            moved = pltpu.roll(packs[s], shift, 1) if shift else packs[s]
            out = moved if out is None else jnp.where(big_group == s, moved, out)
        pieces.append(out.reshape(groups, 1, piece, LANES))
    coefs = jnp.concatenate(pieces, axis=1).reshape(slots, LANES)
    spread = jnp.concatenate(
        [jnp.where(marks == float(l + 1), coefs, 0.0) for l in range(local)], axis=1
    )
    rhs_all = dot3(turned, split(spread), 1, 0)[coef_rows : coef_rows + dates]
    rhs = [
        [split(rhs_all[n : n + half, l * width : (l + 1) * width]) for l in range(local)]
        for n in range(0, dates, half)
    ]
    steps = [h // 2 for h in far_first if h % 2 == 0] + [0]
    cross, sums, solutions = {}, {}, {}
    weight = [[jnp.where(up[l] == p, 1.0, 0.0) for p in range(tops_all)] for l in range(local)]
    for n in range(cuts):
        updates = [dot3(rhs[n][l], (wide[0, l], wide[1, l]), 1, 1) for l in range(local)]
        for p in range(tops_all):
            acc = weight[0][p] * updates[0]
            for l in range(1, local):
                acc = acc + weight[l][p] * updates[l]
            parts[n, p] = acc
        for h in steps:
            copy = pltpu.make_async_remote_copy(
                src_ref=parts.at[n, pl.ds(leaf_peers[2 * h + 1] * top_each, top_each)],
                dst_ref=across.at[n, h],
                send_sem=a_send.at[n, h],
                recv_sem=a_recv.at[n, h],
                device_id=(leaf_peers[1], shard),
                device_id_type=MESH,
            )
            copy.start()
            cross[n, h] = copy
    residue = []
    for n in range(cuts):
        for h in steps:
            cross[n, h].wait_recv()
            here = parts[n, pl.ds(leaf_peers[2 * h] * top_each, top_each)] + across[n, h]
            if h == 0:
                residue.append(trhs[:, n * half : (n + 1) * half] - here)
                continue
            joined[n, h] = here
            copy = pltpu.make_async_remote_copy(
                src_ref=joined.at[n, h],
                dst_ref=along.at[n, h],
                send_sem=z_send.at[n, h],
                recv_sem=z_recv.at[n, h],
                device_id=(leaf_peers[2 * h], shard),
                device_id_type=MESH,
            )
            copy.start()
            sums[n, h] = copy
    for l in range(local):
        factor = split(inv[l])
        for n in range(cuts):
            solved = split(dot3(rhs[n][l], factor, 1, 1))
            base[l, n * half : (n + 1) * half] = dot3(solved, factor, 1, 0)

    def pass_on(n, h, o, peer):
        block = top_out.at[pl.ds(leaf_peers[h] * top_each, top_each), pl.ds(n * half, half)]
        copy = pltpu.make_async_remote_copy(
            src_ref=block,
            dst_ref=block,
            send_sem=g_send.at[n, o],
            recv_sem=g_recv.at[n, o],
            device_id=(leaf_peers[peer], shard),
            device_id_type=MESH,
        )
        copy.start()
        solutions[n, o] = copy

    for n in range(cuts):
        left = residue[n]
        for h in steps[:-1]:
            sums[n, h].wait_recv()
            left = left - along[n, h]
        for i in range(top_each):
            top_out[me * top_each + i, n * half : (n + 1) * half] = dot3(
                split(left[i]), gram[i], 1, 0
            )
        for h in steps[:-1]:
            pass_on(n, 0, 2 * h, 2 * h)
        pass_on(n, 0, 1, 1)
    for n in range(cuts):
        for h in reversed(steps[:-1]):
            solutions[n, 2 * h].wait_recv()
            pass_on(n, 2 * h, 2 * h + 1, 1)
    for copy in [*row_copies.values(), *forwards, *cross.values(), *sums.values()]:
        copy.wait_send()
    for n in range(cuts):
        for h in reversed(steps):
            solutions[n, 2 * h + 1].wait_recv()
        dates_here = slice(n * half, (n + 1) * half)
        for l in range(local):
            own = weight[l][0] * top_out[0, dates_here]
            for p in range(1, tops_all):
                own = own + weight[l][p] * top_out[p, dates_here]
            lifted = dot3(split(own), (wide[0, l], wide[1, l]), 1, 0)
            leaf_out[l, dates_here] = base[l, dates_here] - lifted
    for copy in solutions.values():
        copy.wait_send()


def fused(
    obs_coef, obs_data, obs_target, leaf_map, leaf_parent, leaf_inv, leaf_off, top_inv, top_rhs
):
    groups, shards = lax.axis_size("leaf"), lax.axis_size("rhs")
    rows = obs_target.shape[0]
    capacity = 2 * rows // groups
    local, width = leaf_inv.shape[0], leaf_inv.shape[1]
    top_count, dates = top_inv.shape[0], obs_data.shape[0]
    top_each = top_count // groups
    coef_rows = obs_coef.shape[0]
    piece = capacity * coef_rows // LANES
    pair = groups // 2
    cuts = 2 if dates % 16 == 0 else 1
    half = dates // cuts
    dma = pltpu.SemaphoreType.DMA
    vmem = pl.BlockSpec(memory_space=pltpu.VMEM)
    hbm = pl.BlockSpec(memory_space=pltpu.HBM)
    return pl.pallas_call(
        functools.partial(kernel, groups, shards, capacity),
        out_shape=(
            jax.ShapeDtypeStruct((local, dates, width), F32),
            jax.ShapeDtypeStruct((top_count, dates, width), F32),
        ),
        in_specs=[hbm] * 9,
        out_specs=(vmem, vmem),
        scratch_shapes=[
            pltpu.VMEM((1, rows), jnp.int32),
            pltpu.VMEM(obs_coef.shape, F32),
            pltpu.VMEM(obs_data.shape, F32),
            pltpu.SMEM(leaf_map.shape, jnp.int32),
            pltpu.SMEM(leaf_parent.shape, jnp.int32),
            pltpu.VMEM(leaf_inv.shape, F32),
            pltpu.VMEM(leaf_off.shape, F32),
            pltpu.VMEM((top_each, width, width), F32),
            pltpu.VMEM((top_each, dates, width), F32),
            pltpu.VMEM((groups, capacity, LANES), F32),
            pltpu.VMEM((groups, capacity, LANES), F32),
            pltpu.VMEM((shards, groups, piece, LANES), F32),
            pltpu.VMEM((2, local, width, width), BF16),
            pltpu.VMEM((local, dates, width), F32),
            pltpu.VMEM((cuts, top_count, half, width), F32),
            pltpu.VMEM((cuts, groups // 2, top_each, half, width), F32),
            pltpu.VMEM((cuts, groups // 2, top_each, half, width), F32),
            pltpu.VMEM((cuts, groups // 2, top_each, half, width), F32),
            dma((groups,)),
            dma((groups,)),
            dma((shards, pair)),
            dma((shards, pair)),
            dma((cuts, groups // 2)),
            dma((cuts, groups // 2)),
            dma((cuts, groups // 2)),
            dma((cuts, groups // 2)),
            dma((cuts, groups)),
            dma((cuts, groups)),
            dma((9,)),
        ],
        compiler_params=pltpu.CompilerParams(
            collective_id=0, has_side_effects=True, vmem_limit_bytes=24 * 2**20
        ),
    )(
        *(
            pltpu.with_memory_space_constraint(x, pltpu.HBM)
            for x in (
                obs_target.reshape(1, rows), obs_coef, obs_data, leaf_map, leaf_parent,
                leaf_inv, leaf_off, top_inv, top_rhs,
            )
        )
    )


def plain(
    obs_coef, obs_data, obs_target, leaf_map, leaf_parent, leaf_inv, leaf_off, top_inv, top_rhs
):
    highest = lax.Precision.HIGHEST
    groups = lax.axis_size("leaf")
    device_index = lax.axis_index("leaf")
    local_count = leaf_inv.shape[0]
    block_width = leaf_inv.shape[1]
    top_count = top_inv.shape[0]
    date_cols = obs_data.shape[0]
    rows_here = obs_target.shape[0]
    leaf_total = leaf_map.shape[0]
    capacity = max(2, 2 * rows_here // groups)
    slots_total = groups * capacity
    all_ids = jnp.arange(leaf_total, dtype=jnp.int32)
    id_match = obs_target[:, None] == all_ids[None, :]
    position = jnp.sum(jnp.where(id_match, leaf_map[None, :], 0), axis=1)
    owner_dev = position // local_count
    member = position % local_count
    row_ids = jnp.arange(rows_here, dtype=jnp.int32)
    earlier = (owner_dev[:, None] == owner_dev[None, :]) & (row_ids[:, None] > row_ids[None, :])
    queue_rank = jnp.sum(earlier.astype(jnp.int32), axis=1)
    target_slot = owner_dev * capacity + queue_rank
    slot_mark = (member + 1).astype(jnp.float32)[None, :]
    fields = jnp.concatenate([obs_coef, obs_data, slot_mark], axis=0)
    placed = jnp.zeros((fields.shape[0], slots_total), F32).at[:, target_slot].set(fields)
    received = lax.all_to_all(placed, "leaf", split_axis=1, concat_axis=1, tiled=True)
    part_coef = received[: obs_coef.shape[0]]
    recv_data = received[obs_coef.shape[0] : -1]
    recv_mark = received[-1:]
    recv_coef = lax.all_gather(part_coef, "rhs", axis=0, tiled=True)
    slot_values = (jnp.arange(local_count, dtype=jnp.int32) + 1).astype(jnp.float32)
    chosen = (recv_mark[0][None, :] == slot_values[:, None]).astype(jnp.float32)
    spread = (recv_data[None, :, :] * chosen[:, None, :]).reshape(
        local_count * date_cols, slots_total
    )
    leaf_rhs = lax.dot_general(
        spread, recv_coef, (((1,), (1,)), ((), ())), precision=highest
    ).reshape(local_count, date_cols, block_width)
    solved = jnp.einsum("ltc,ldc->ltd", leaf_rhs, leaf_inv, precision=highest)
    update = jnp.einsum("ltd,lcd->ltc", solved, leaf_off, precision=highest)
    positions_here = device_index * local_count + jnp.arange(local_count, dtype=jnp.int32)
    holder_match = leaf_map[None, :] == positions_here[:, None]
    parent_here = jnp.sum(jnp.where(holder_match, leaf_parent[None, :], 0), axis=1)
    to_top = (parent_here[:, None] == jnp.arange(top_count, dtype=jnp.int32)[None, :]).astype(
        jnp.float32
    )
    contrib = jnp.einsum("lp,ltc->ptc", to_top, update, precision=highest)
    flat_terms = contrib.reshape(top_count * date_cols, block_width)
    top_total = lax.psum(flat_terms, "leaf").reshape(top_count, date_cols, block_width)
    residue = top_rhs - top_total
    top_solved = jnp.einsum("ptc,pdc->ptd", residue, top_inv, precision=highest)
    top_solution = jnp.einsum("ptd,pdc->ptc", top_solved, top_inv, precision=highest)
    from_top = jnp.einsum("lp,ptc->ltc", to_top, top_solution, precision=highest)
    lifted = jnp.einsum("ltc,lcd->ltd", from_top, leaf_off, precision=highest)
    leaf_solution = jnp.einsum("ltc,lcd->ltd", solved - lifted, leaf_inv, precision=highest)
    return (leaf_solution, top_solution)


def body(*args):
    obs_coef, obs_data, obs_target = args[:3]
    groups = lax.axis_size("leaf")
    coef_rows, rows = obs_coef.shape
    dates = obs_data.shape[0]
    fits = (
        args[7].shape[0] % groups == 0
        and groups > 1
        and groups & (groups - 1) == 0
        and rows % LANES == 0
        and (2 * rows) % groups == 0
        and LANES % coef_rows == 0
        and (2 * rows // groups) % (8 * (LANES // coef_rows)) == 0
        and coef_rows % 8 == 0
        and dates % 8 == 0
        and coef_rows + dates < LANES
        and args[5].shape[1] == LANES
    )
    return fused(*args) if fits else plain(*args)


def solution(mesh):
    return jax.shard_map(
        body,
        mesh=mesh,
        in_specs=(
            P("rhs", "leaf"),
            P("rhs", "leaf"),
            P("leaf"),
            P(),
            P(),
            P("leaf", None, None),
            P("leaf", None, None),
            P(),
            P(None, "rhs", None),
        ),
        out_specs=(P("leaf", "rhs", None), P(None, "rhs", None)),
        check_vma=False,
    )
```

```python
import functools

import jax
import jax.numpy as jnp
from jax import lax
from jax.experimental import pallas as pl
from jax.experimental.pallas import tpu as pltpu
from jax.sharding import PartitionSpec as P

F32, BF16 = jnp.float32, jnp.bfloat16
MESH = pl.DeviceIdType.MESH
LANES = 128


def split(x):
    high = x.astype(BF16)
    return high, (x - high.astype(F32)).astype(BF16)


def contract(a, b, ca, cb):
    return lax.dot_general(a, b, (((ca,), (cb,)), ((), ())), preferred_element_type=F32)


def dot3(a, b, ca, cb):
    (ah, al), (bh, bl) = a, b
    return contract(ah, bh, ca, cb) + (contract(ah, bl, ca, cb) + contract(al, bh, ca, cb))


def flipped(index, bits, count):
    out = index
    place = 1
    while place < count:
        if bits & place:
            out = out + place * (1 - 2 * lax.rem(lax.div(index, place), 2))
        place *= 2
    return out


def kernel(
    groups, shards, capacity,
    tgt_h, coef_h, data_h, lmap_h, lpar_h, inv_h, off_h, tinv_h, trhs_h,
    leaf_out, top_out,
    tgt, coef, data, lmap, lpar, inv, off, tinv, trhs,
    send, recv, packed, wide, base, parts, across, joined, along,
    d_send, d_recv, f_send, f_recv, a_send, a_recv, z_send, z_recv, g_send, g_recv, l_sem,
):
    me = lax.axis_index("leaf")
    shard = lax.axis_index("rhs")
    local, width = inv.shape[0], inv.shape[1]
    coef_rows, rows = coef.shape
    dates = data.shape[0]
    top_each = tinv.shape[0]
    total = lmap.shape[0]
    fold = LANES // coef_rows
    piece = capacity // fold
    pair = f_send.shape[1]
    cuts, tops_all, half = parts.shape[0], parts.shape[1], parts.shape[2]
    per = groups // pair
    leaf_peers = [flipped(me, o, groups) for o in range(groups)]
    far_first = sorted(range(1, groups), key=lambda o: (-(o.bit_length()), o))
    rhs_peers = [lax.rem(shard + o, shards) for o in range(shards)]

    barrier = pltpu.get_barrier_semaphore()
    for o in range(1, groups):
        pl.semaphore_signal(barrier, inc=1, device_id=(leaf_peers[o], shard), device_id_type=MESH)
    for o in range(1, shards):
        pl.semaphore_signal(barrier, inc=1, device_id=(me, rhs_peers[o]), device_id_type=MESH)
    tops = pl.ds(me * top_each, top_each)
    loads = []
    for i, (src, dst) in enumerate(
        [
            (tgt_h, tgt),
            (lmap_h, lmap),
            (coef_h, coef),
            (data_h, data),
            (lpar_h, lpar),
            (inv_h, inv),
            (off_h, off),
            (tinv_h.at[tops], tinv),
            (trhs_h.at[tops], trhs),
        ]
    ):
        copy = pltpu.make_async_copy(src, dst, l_sem.at[i])
        copy.start()
        loads.append(copy)
    loads[0].wait()
    loads[1].wait()

    target = tgt[...]
    position = jnp.zeros_like(target)
    for i in range(total):
        position = jnp.where(target == i, lmap[i], position)
    place = lax.broadcasted_iota(jnp.int32, (groups, rows), 0)
    first = jnp.zeros_like(place)
    for o in range(groups):
        first = jnp.where(place == o, leaf_peers[o] * local, first)
    member = jnp.broadcast_to(position, (groups, rows)) - first
    owned = (member >= 0) & (member < local)
    hot = jnp.where(owned, 1.0, 0.0)
    before = (
        lax.broadcasted_iota(jnp.int32, (rows, rows), 0)
        < lax.broadcasted_iota(jnp.int32, (rows, rows), 1)
    )
    rank = contract(hot.astype(BF16), jnp.where(before, 1.0, 0.0).astype(BF16), 1, 0)
    slot = jnp.where(owned, rank.astype(jnp.int32), -1)
    mark = jnp.sum(hot * (member + 1).astype(F32), axis=0, keepdims=True)
    slot_ids = lax.broadcasted_iota(jnp.int32, (capacity, rows), 0)
    loads[2].wait()
    loads[3].wait()
    fields = jnp.concatenate(
        [
            coef[...],
            data[...],
            jnp.broadcast_to(mark, (LANES - coef_rows - dates, rows)),
        ],
        axis=0,
    )
    high, low = split(fields)

    def placed(o):
        chosen = jnp.where(slot_ids == slot[o : o + 1, :], 1.0, 0.0).astype(BF16)
        return contract(chosen, high, 1, 1) + contract(chosen, low, 1, 1)

    pl.semaphore_wait(barrier, groups - 1 + shards - 1)
    row_copies = {}
    for o in far_first:
        send[o] = placed(o)
        copy = pltpu.make_async_remote_copy(
            src_ref=send.at[o],
            dst_ref=recv.at[o],
            send_sem=d_send.at[o],
            recv_sem=d_recv.at[o],
            device_id=(leaf_peers[o], shard),
            device_id_type=MESH,
        )
        copy.start()
        row_copies[o] = copy
    recv[0] = placed(0)

    for copy in loads[4:]:
        copy.wait()
    for l in range(local):
        high, low = split(dot3(split(off[l]), split(inv[l]), 1, 0))
        wide[0, l] = high
        wide[1, l] = low
    gram = []
    for i in range(top_each):
        block = split(tinv[i])
        gram.append(split(dot3(block, block, 0, 0)))
    up = []
    for l in range(local):
        found = jnp.int32(0)
        for i in range(total):
            found = jnp.where(lmap[i] == me * local + l, lpar[i], found)
        up.append(found)

    lane_group = lax.broadcasted_iota(jnp.int32, (piece, LANES), 1) // coef_rows
    forwards = []
    for g in range(pair):
        for o in range(g * per, (g + 1) * per):
            if o > 0:
                row_copies[o].wait_recv()
            block = recv[o]
            out = block[:piece]
            for q in range(1, fold):
                moved = pltpu.roll(block[q * piece : (q + 1) * piece], q * coef_rows, 1)
                out = jnp.where(lane_group == q, moved, out)
            packed[shard, o] = out
        span = pl.ds(g * per, per)
        for o in range(1, shards):
            copy = pltpu.make_async_remote_copy(
                src_ref=packed.at[shard, span],
                dst_ref=packed.at[shard, span],
                send_sem=f_send.at[o, g],
                recv_sem=f_recv.at[o, g],
                device_id=(me, rhs_peers[o]),
                device_id_type=MESH,
            )
            copy.start()
            forwards.append(copy)
    ready = len(forwards) // 2
    span = groups // 2
    big_group = lax.broadcasted_iota(jnp.int32, (span * piece, LANES), 1) // coef_rows
    rhs_all = None
    for part in range(2):
        here = slice(part * span, (part + 1) * span)
        rows_in = recv[here].reshape(span * capacity, LANES)
        turned = split(rows_in.T)
        marks = rows_in[:, coef_rows + dates : coef_rows + dates + 1]
        for copy in forwards[part * ready : (part + 1) * ready]:
            copy.wait_recv()
        packs = [packed[s, here].reshape(span * piece, LANES) for s in range(shards)]
        pieces = []
        for q in range(fold):
            out = None
            for s in range(shards):
                shift = ((s - q) * coef_rows) % LANES
                moved = pltpu.roll(packs[s], shift, 1) if shift else packs[s]
                out = moved if out is None else jnp.where(big_group == s, moved, out)
            pieces.append(out.reshape(span, 1, piece, LANES))
        coefs = jnp.concatenate(pieces, axis=1).reshape(span * capacity, LANES)
        spread = jnp.concatenate(
            [jnp.where(marks == float(l + 1), coefs, 0.0) for l in range(local)], axis=1
        )
        term = dot3(turned, split(spread), 1, 0)[coef_rows : coef_rows + dates]
        rhs_all = term if rhs_all is None else rhs_all + term
    rhs = [
        [split(rhs_all[n : n + half, l * width : (l + 1) * width]) for l in range(local)]
        for n in range(0, dates, half)
    ]
    steps = [h // 2 for h in far_first if h % 2 == 0] + [0]
    cross, sums, solutions = {}, {}, {}
    weight = [[jnp.where(up[l] == p, 1.0, 0.0) for p in range(tops_all)] for l in range(local)]
    for n in range(cuts):
        updates = [dot3(rhs[n][l], (wide[0, l], wide[1, l]), 1, 1) for l in range(local)]
        for p in range(tops_all):
            acc = weight[0][p] * updates[0]
            for l in range(1, local):
                acc = acc + weight[l][p] * updates[l]
            parts[n, p] = acc
        for h in steps:
            copy = pltpu.make_async_remote_copy(
                src_ref=parts.at[n, pl.ds(leaf_peers[2 * h + 1] * top_each, top_each)],
                dst_ref=across.at[n, h],
                send_sem=a_send.at[n, h],
                recv_sem=a_recv.at[n, h],
                device_id=(leaf_peers[1], shard),
                device_id_type=MESH,
            )
            copy.start()
            cross[n, h] = copy
    residue = []
    for n in range(cuts):
        for h in steps:
            cross[n, h].wait_recv()
            here = parts[n, pl.ds(leaf_peers[2 * h] * top_each, top_each)] + across[n, h]
            if h == 0:
                residue.append(trhs[:, n * half : (n + 1) * half] - here)
                continue
            joined[n, h] = here
            copy = pltpu.make_async_remote_copy(
                src_ref=joined.at[n, h],
                dst_ref=along.at[n, h],
                send_sem=z_send.at[n, h],
                recv_sem=z_recv.at[n, h],
                device_id=(leaf_peers[2 * h], shard),
                device_id_type=MESH,
            )
            copy.start()
            sums[n, h] = copy
    for l in range(local):
        factor = split(inv[l])
        for n in range(cuts):
            solved = split(dot3(rhs[n][l], factor, 1, 1))
            base[l, n * half : (n + 1) * half] = dot3(solved, factor, 1, 0)

    def pass_on(n, h, o, peer):
        block = top_out.at[pl.ds(leaf_peers[h] * top_each, top_each), pl.ds(n * half, half)]
        copy = pltpu.make_async_remote_copy(
            src_ref=block,
            dst_ref=block,
            send_sem=g_send.at[n, o],
            recv_sem=g_recv.at[n, o],
            device_id=(leaf_peers[peer], shard),
            device_id_type=MESH,
        )
        copy.start()
        solutions[n, o] = copy

    for n in range(cuts):
        left = residue[n]
        for h in steps[:-1]:
            sums[n, h].wait_recv()
            left = left - along[n, h]
        for i in range(top_each):
            top_out[me * top_each + i, n * half : (n + 1) * half] = dot3(
                split(left[i]), gram[i], 1, 0
            )
        for h in steps[:-1]:
            pass_on(n, 0, 2 * h, 2 * h)
        pass_on(n, 0, 1, 1)
    for n in range(cuts):
        for h in reversed(steps[:-1]):
            solutions[n, 2 * h].wait_recv()
            pass_on(n, 2 * h, 2 * h + 1, 1)
    for copy in [*row_copies.values(), *forwards, *cross.values(), *sums.values()]:
        copy.wait_send()
    for n in range(cuts):
        for h in reversed(steps):
            solutions[n, 2 * h + 1].wait_recv()
        dates_here = slice(n * half, (n + 1) * half)
        for l in range(local):
            own = weight[l][0] * top_out[0, dates_here]
            for p in range(1, tops_all):
                own = own + weight[l][p] * top_out[p, dates_here]
            lifted = dot3(split(own), (wide[0, l], wide[1, l]), 1, 0)
            leaf_out[l, dates_here] = base[l, dates_here] - lifted
    for copy in solutions.values():
        copy.wait_send()


def write_out(leaf_v, top_v, leaf_h, top_h, sems):
    copies = [
        pltpu.make_async_copy(leaf_v, leaf_h, sems.at[0]),
        pltpu.make_async_copy(top_v, top_h, sems.at[1]),
    ]
    for copy in copies:
        copy.start()
    for copy in copies:
        copy.wait()


def fused(
    obs_coef, obs_data, obs_target, leaf_map, leaf_parent, leaf_inv, leaf_off, top_inv, top_rhs
):
    groups, shards = lax.axis_size("leaf"), lax.axis_size("rhs")
    rows = obs_target.shape[0]
    capacity = 2 * rows // groups
    local, width = leaf_inv.shape[0], leaf_inv.shape[1]
    top_count, dates = top_inv.shape[0], obs_data.shape[0]
    top_each = top_count // groups
    coef_rows = obs_coef.shape[0]
    piece = capacity * coef_rows // LANES
    pair = groups // 2
    cuts = 2 if dates % 16 == 0 else 1
    half = dates // cuts
    dma = pltpu.SemaphoreType.DMA
    vmem = pl.BlockSpec(memory_space=pltpu.VMEM)
    hbm = pl.BlockSpec(memory_space=pltpu.HBM)
    results = (
        jax.ShapeDtypeStruct((local, dates, width), F32),
        jax.ShapeDtypeStruct((top_count, dates, width), F32),
    )
    solved = pl.pallas_call(
        functools.partial(kernel, groups, shards, capacity),
        out_shape=results,
        in_specs=[hbm] * 9,
        out_specs=(vmem, vmem),
        scratch_shapes=[
            pltpu.VMEM((1, rows), jnp.int32),
            pltpu.VMEM(obs_coef.shape, F32),
            pltpu.VMEM(obs_data.shape, F32),
            pltpu.SMEM(leaf_map.shape, jnp.int32),
            pltpu.SMEM(leaf_parent.shape, jnp.int32),
            pltpu.VMEM(leaf_inv.shape, F32),
            pltpu.VMEM(leaf_off.shape, F32),
            pltpu.VMEM((top_each, width, width), F32),
            pltpu.VMEM((top_each, dates, width), F32),
            pltpu.VMEM((groups, capacity, LANES), F32),
            pltpu.VMEM((groups, capacity, LANES), F32),
            pltpu.VMEM((shards, groups, piece, LANES), F32),
            pltpu.VMEM((2, local, width, width), BF16),
            pltpu.VMEM((local, dates, width), F32),
            pltpu.VMEM((cuts, top_count, half, width), F32),
            pltpu.VMEM((cuts, groups // 2, top_each, half, width), F32),
            pltpu.VMEM((cuts, groups // 2, top_each, half, width), F32),
            pltpu.VMEM((cuts, groups // 2, top_each, half, width), F32),
            dma((groups,)),
            dma((groups,)),
            dma((shards, pair)),
            dma((shards, pair)),
            dma((cuts, groups // 2)),
            dma((cuts, groups // 2)),
            dma((cuts, groups // 2)),
            dma((cuts, groups // 2)),
            dma((cuts, groups)),
            dma((cuts, groups)),
            dma((9,)),
        ],
        compiler_params=pltpu.CompilerParams(
            collective_id=0, has_side_effects=True, vmem_limit_bytes=24 * 2**20
        ),
    )(
        *(
            pltpu.with_memory_space_constraint(x, pltpu.HBM)
            for x in (
                obs_target.reshape(1, rows), obs_coef, obs_data, leaf_map, leaf_parent,
                leaf_inv, leaf_off, top_inv, top_rhs,
            )
        )
    )
    return pl.pallas_call(
        write_out,
        out_shape=results,
        in_specs=[vmem, vmem],
        out_specs=(hbm, hbm),
        scratch_shapes=[dma((2,))],
        compiler_params=pltpu.CompilerParams(vmem_limit_bytes=4 * 2**20),
    )(*solved)


def plain(
    obs_coef, obs_data, obs_target, leaf_map, leaf_parent, leaf_inv, leaf_off, top_inv, top_rhs
):
    highest = lax.Precision.HIGHEST
    groups = lax.axis_size("leaf")
    device_index = lax.axis_index("leaf")
    local_count = leaf_inv.shape[0]
    block_width = leaf_inv.shape[1]
    top_count = top_inv.shape[0]
    date_cols = obs_data.shape[0]
    rows_here = obs_target.shape[0]
    leaf_total = leaf_map.shape[0]
    capacity = max(2, 2 * rows_here // groups)
    slots_total = groups * capacity
    all_ids = jnp.arange(leaf_total, dtype=jnp.int32)
    id_match = obs_target[:, None] == all_ids[None, :]
    position = jnp.sum(jnp.where(id_match, leaf_map[None, :], 0), axis=1)
    owner_dev = position // local_count
    member = position % local_count
    row_ids = jnp.arange(rows_here, dtype=jnp.int32)
    earlier = (owner_dev[:, None] == owner_dev[None, :]) & (row_ids[:, None] > row_ids[None, :])
    queue_rank = jnp.sum(earlier.astype(jnp.int32), axis=1)
    target_slot = owner_dev * capacity + queue_rank
    slot_mark = (member + 1).astype(jnp.float32)[None, :]
    fields = jnp.concatenate([obs_coef, obs_data, slot_mark], axis=0)
    placed = jnp.zeros((fields.shape[0], slots_total), F32).at[:, target_slot].set(fields)
    received = lax.all_to_all(placed, "leaf", split_axis=1, concat_axis=1, tiled=True)
    part_coef = received[: obs_coef.shape[0]]
    recv_data = received[obs_coef.shape[0] : -1]
    recv_mark = received[-1:]
    recv_coef = lax.all_gather(part_coef, "rhs", axis=0, tiled=True)
    slot_values = (jnp.arange(local_count, dtype=jnp.int32) + 1).astype(jnp.float32)
    chosen = (recv_mark[0][None, :] == slot_values[:, None]).astype(jnp.float32)
    spread = (recv_data[None, :, :] * chosen[:, None, :]).reshape(
        local_count * date_cols, slots_total
    )
    leaf_rhs = lax.dot_general(
        spread, recv_coef, (((1,), (1,)), ((), ())), precision=highest
    ).reshape(local_count, date_cols, block_width)
    solved = jnp.einsum("ltc,ldc->ltd", leaf_rhs, leaf_inv, precision=highest)
    update = jnp.einsum("ltd,lcd->ltc", solved, leaf_off, precision=highest)
    positions_here = device_index * local_count + jnp.arange(local_count, dtype=jnp.int32)
    holder_match = leaf_map[None, :] == positions_here[:, None]
    parent_here = jnp.sum(jnp.where(holder_match, leaf_parent[None, :], 0), axis=1)
    to_top = (parent_here[:, None] == jnp.arange(top_count, dtype=jnp.int32)[None, :]).astype(
        jnp.float32
    )
    contrib = jnp.einsum("lp,ltc->ptc", to_top, update, precision=highest)
    flat_terms = contrib.reshape(top_count * date_cols, block_width)
    top_total = lax.psum(flat_terms, "leaf").reshape(top_count, date_cols, block_width)
    residue = top_rhs - top_total
    top_solved = jnp.einsum("ptc,pdc->ptd", residue, top_inv, precision=highest)
    top_solution = jnp.einsum("ptd,pdc->ptc", top_solved, top_inv, precision=highest)
    from_top = jnp.einsum("lp,ptc->ltc", to_top, top_solution, precision=highest)
    lifted = jnp.einsum("ltc,lcd->ltd", from_top, leaf_off, precision=highest)
    leaf_solution = jnp.einsum("ltc,lcd->ltd", solved - lifted, leaf_inv, precision=highest)
    return (leaf_solution, top_solution)


def body(*args):
    obs_coef, obs_data, obs_target = args[:3]
    groups = lax.axis_size("leaf")
    coef_rows, rows = obs_coef.shape
    dates = obs_data.shape[0]
    fits = (
        args[7].shape[0] % groups == 0
        and groups > 1
        and groups & (groups - 1) == 0
        and rows % LANES == 0
        and (2 * rows) % groups == 0
        and LANES % coef_rows == 0
        and (2 * rows // groups) % (8 * (LANES // coef_rows)) == 0
        and coef_rows % 8 == 0
        and dates % 8 == 0
        and coef_rows + dates < LANES
        and args[5].shape[1] == LANES
    )
    return fused(*args) if fits else plain(*args)


def solution(mesh):
    return jax.shard_map(
        body,
        mesh=mesh,
        in_specs=(
            P("rhs", "leaf"),
            P("rhs", "leaf"),
            P("leaf"),
            P(),
            P(),
            P("leaf", None, None),
            P("leaf", None, None),
            P(),
            P(None, "rhs", None),
        ),
        out_specs=(P("leaf", "rhs", None), P(None, "rhs", None)),
        check_vma=False,
    )
```

```python
import functools

import jax
import jax.numpy as jnp
from jax import lax
from jax.experimental import pallas as pl
from jax.experimental.pallas import tpu as pltpu
from jax.sharding import PartitionSpec as P

F32, BF16 = jnp.float32, jnp.bfloat16
MESH = pl.DeviceIdType.MESH
LANES = 128


def split(x):
    high = x.astype(BF16)
    return high, (x - high.astype(F32)).astype(BF16)


def contract(a, b, ca, cb):
    return lax.dot_general(a, b, (((ca,), (cb,)), ((), ())), preferred_element_type=F32)


def dot3(a, b, ca, cb):
    (ah, al), (bh, bl) = a, b
    return contract(ah, bh, ca, cb) + (contract(ah, bl, ca, cb) + contract(al, bh, ca, cb))


def flipped(index, bits, count):
    out = index
    place = 1
    while place < count:
        if bits & place:
            out = out + place * (1 - 2 * lax.rem(lax.div(index, place), 2))
        place *= 2
    return out


def kernel(
    groups, shards, capacity,
    tgt_h, coef_h, data_h, lmap_h, lpar_h, inv_h, off_h, tinv_h, trhs_h,
    leaf_out, top_out,
    tgt, coef, data, lmap, lpar, inv, off, tinv, trhs,
    send, recv, packed, wide, base, parts, across, joined, along,
    d_send, d_recv, f_send, f_recv, a_send, a_recv, z_send, z_recv, g_send, g_recv, l_sem,
):
    me = lax.axis_index("leaf")
    shard = lax.axis_index("rhs")
    local, width = inv.shape[0], inv.shape[1]
    coef_rows, rows = coef.shape
    dates = data.shape[0]
    top_each = tinv.shape[0]
    total = lmap.shape[0]
    fold = LANES // coef_rows
    piece = capacity // fold
    pair = f_send.shape[1]
    cuts, tops_all, half = parts.shape[0], parts.shape[1], parts.shape[2]
    per = groups // pair
    leaf_peers = [flipped(me, o, groups) for o in range(groups)]
    far_first = sorted(range(1, groups), key=lambda o: (-(o.bit_length()), o))
    order = [0]
    for o in range(groups // 2):
        order += [groups // 2 + o] + ([o + 1] if o + 1 < groups // 2 else [])
    rhs_peers = [lax.rem(shard + o, shards) for o in range(shards)]

    barrier = pltpu.get_barrier_semaphore()
    for o in range(1, groups):
        pl.semaphore_signal(barrier, inc=1, device_id=(leaf_peers[o], shard), device_id_type=MESH)
    for o in range(1, shards):
        pl.semaphore_signal(barrier, inc=1, device_id=(me, rhs_peers[o]), device_id_type=MESH)
    tops = pl.ds(me * top_each, top_each)
    loads = []
    for i, (src, dst) in enumerate(
        [
            (tgt_h, tgt),
            (lmap_h, lmap),
            (coef_h, coef),
            (data_h, data),
            (lpar_h, lpar),
            (inv_h, inv),
            (off_h, off),
            (tinv_h.at[tops], tinv),
            (trhs_h.at[tops], trhs),
        ]
    ):
        copy = pltpu.make_async_copy(src, dst, l_sem.at[i])
        copy.start()
        loads.append(copy)
    loads[0].wait()
    loads[1].wait()

    target = tgt[...]
    position = jnp.zeros_like(target)
    for i in range(total):
        position = jnp.where(target == i, lmap[i], position)
    place = lax.broadcasted_iota(jnp.int32, (groups, rows), 0)
    first = jnp.zeros_like(place)
    for o in range(groups):
        first = jnp.where(place == o, leaf_peers[o] * local, first)
    member = jnp.broadcast_to(position, (groups, rows)) - first
    owned = (member >= 0) & (member < local)
    hot = jnp.where(owned, 1.0, 0.0)
    before = (
        lax.broadcasted_iota(jnp.int32, (rows, rows), 0)
        < lax.broadcasted_iota(jnp.int32, (rows, rows), 1)
    )
    rank = contract(hot.astype(BF16), jnp.where(before, 1.0, 0.0).astype(BF16), 1, 0)
    slot = jnp.where(owned, rank.astype(jnp.int32), -1)
    mark = jnp.sum(hot * (member + 1).astype(F32), axis=0, keepdims=True)
    slot_ids = lax.broadcasted_iota(jnp.int32, (capacity, rows), 0)
    loads[2].wait()
    loads[3].wait()
    gap = lambda n: [jnp.zeros((n, rows), F32)] if n else []
    coef_fields = split(
        jnp.concatenate(
            [
                jnp.concatenate(
                    gap(q * coef_rows) + [coef[...]] + gap((fold - 1 - q) * coef_rows), axis=0
                )
                for q in range(fold)
            ],
            axis=1,
        )
    )
    marks = jnp.broadcast_to(mark, (8, rows))
    date_fields = split(
        jnp.concatenate(
            [
                jnp.concatenate([data[: dates // 2], marks], axis=0),
                jnp.concatenate([data[dates // 2 :], marks], axis=0),
            ],
            axis=1,
        )
    )

    def place_rows(o, i):
        chosen = jnp.where(slot_ids == slot[o : o + 1, :], 1.0, 0.0)
        folded = jnp.concatenate(
            [chosen[q * piece : (q + 1) * piece] for q in range(fold)], axis=1
        ).astype(BF16)
        none = jnp.zeros_like(chosen)
        doubled = jnp.concatenate(
            [
                jnp.concatenate([chosen, none], axis=1),
                jnp.concatenate([none, chosen], axis=1),
            ],
            axis=0,
        ).astype(BF16)
        send[i, :piece] = contract(folded, coef_fields[0], 1, 1) + contract(
            folded, coef_fields[1], 1, 1
        )
        send[i, piece:] = contract(date_fields[0], doubled, 1, 1) + contract(
            date_fields[1], doubled, 1, 1
        )

    pl.semaphore_wait(barrier, groups - 1 + shards - 1)
    row_copies = {}
    for i in range(1, groups):
        o = order[i]
        place_rows(o, i)
        copy = pltpu.make_async_remote_copy(
            src_ref=send.at[i],
            dst_ref=recv.at[i],
            send_sem=d_send.at[i],
            recv_sem=d_recv.at[i],
            device_id=(leaf_peers[o], shard),
            device_id_type=MESH,
        )
        copy.start()
        row_copies[i] = copy
    place_rows(0, 0)
    recv[0] = send[0]

    for copy in loads[4:]:
        copy.wait()
    for l in range(local):
        high, low = split(dot3(split(off[l]), split(inv[l]), 1, 0))
        wide[0, l] = high
        wide[1, l] = low
    gram = []
    for i in range(top_each):
        block = split(tinv[i])
        gram.append(split(dot3(block, block, 0, 0)))
    up = []
    for l in range(local):
        found = jnp.int32(0)
        for i in range(total):
            found = jnp.where(lmap[i] == me * local + l, lpar[i], found)
        up.append(found)

    forwards = []
    for g in range(pair):
        for i in range(g * per, (g + 1) * per):
            if i > 0:
                row_copies[i].wait_recv()
            packed[shard, i] = recv[i, :piece]
        span = pl.ds(g * per, per)
        for o in range(1, shards):
            copy = pltpu.make_async_remote_copy(
                src_ref=recv.at[span, pl.ds(0, piece)],
                dst_ref=packed.at[shard, span],
                send_sem=f_send.at[o, g],
                recv_sem=f_recv.at[o, g],
                device_id=(me, rhs_peers[o]),
                device_id_type=MESH,
            )
            copy.start()
            forwards.append(copy)
    ready = len(forwards) // 2
    span = groups // 2
    big_group = lax.broadcasted_iota(jnp.int32, (span * piece, LANES), 1) // coef_rows
    rhs_all = None
    first_half = lax.broadcasted_iota(jnp.int32, (recv.shape[1] - piece, LANES), 1) < capacity
    for part in range(2):
        here = slice(part * span, (part + 1) * span)
        series, marked = [], []
        for i in range(part * span, (part + 1) * span, 2):
            one, two = recv[i, piece:], recv[i + 1, piece:]
            early = jnp.where(first_half, one, pltpu.roll(two, capacity, 1))
            late = jnp.where(first_half, pltpu.roll(one, capacity, 1), two)
            series.append(jnp.concatenate([early[: dates // 2], late[: dates // 2]], axis=0))
            marked.append(early[dates // 2 : dates // 2 + 1])
        series = jnp.concatenate(series, axis=1)
        marked = jnp.concatenate(marked, axis=1)
        spread = split(
            jnp.concatenate(
                [jnp.where(marked == float(l + 1), series, 0.0) for l in range(local)], axis=0
            )
        )
        for copy in forwards[part * ready : (part + 1) * ready]:
            copy.wait_recv()
        packs = [packed[s, here].reshape(span * piece, LANES) for s in range(shards)]
        pieces = []
        for q in range(fold):
            out = None
            for s in range(shards):
                shift = ((s - q) * coef_rows) % LANES
                moved = pltpu.roll(packs[s], shift, 1) if shift else packs[s]
                out = moved if out is None else jnp.where(big_group == s, moved, out)
            pieces.append(out.reshape(span, 1, piece, LANES))
        coefs = jnp.concatenate(pieces, axis=1).reshape(span * capacity, LANES)
        term = dot3(spread, split(coefs), 1, 0)
        rhs_all = term if rhs_all is None else rhs_all + term
    rhs = [
        [split(rhs_all[l * dates + n : l * dates + n + half]) for l in range(local)]
        for n in range(0, dates, half)
    ]
    steps = [h // 2 for h in far_first if h % 2 == 0] + [0]
    cross, sums, solutions = {}, {}, {}
    weight = [[jnp.where(up[l] == p, 1.0, 0.0) for p in range(tops_all)] for l in range(local)]
    for n in range(cuts):
        updates = [dot3(rhs[n][l], (wide[0, l], wide[1, l]), 1, 1) for l in range(local)]
        for p in range(tops_all):
            acc = weight[0][p] * updates[0]
            for l in range(1, local):
                acc = acc + weight[l][p] * updates[l]
            parts[n, p] = acc
        for h in steps:
            copy = pltpu.make_async_remote_copy(
                src_ref=parts.at[n, pl.ds(leaf_peers[2 * h + 1] * top_each, top_each)],
                dst_ref=across.at[n, h],
                send_sem=a_send.at[n, h],
                recv_sem=a_recv.at[n, h],
                device_id=(leaf_peers[1], shard),
                device_id_type=MESH,
            )
            copy.start()
            cross[n, h] = copy
    residue = []
    for n in range(cuts):
        for h in steps:
            cross[n, h].wait_recv()
            here = parts[n, pl.ds(leaf_peers[2 * h] * top_each, top_each)] + across[n, h]
            if h == 0:
                residue.append(trhs[:, n * half : (n + 1) * half] - here)
                continue
            joined[n, h] = here
            copy = pltpu.make_async_remote_copy(
                src_ref=joined.at[n, h],
                dst_ref=along.at[n, h],
                send_sem=z_send.at[n, h],
                recv_sem=z_recv.at[n, h],
                device_id=(leaf_peers[2 * h], shard),
                device_id_type=MESH,
            )
            copy.start()
            sums[n, h] = copy
    for l in range(local):
        factor = split(inv[l])
        for n in range(cuts):
            solved = split(dot3(rhs[n][l], factor, 1, 1))
            base[l, n * half : (n + 1) * half] = dot3(solved, factor, 1, 0)

    def pass_on(n, h, o, peer):
        block = top_out.at[pl.ds(leaf_peers[h] * top_each, top_each), pl.ds(n * half, half)]
        copy = pltpu.make_async_remote_copy(
            src_ref=block,
            dst_ref=block,
            send_sem=g_send.at[n, o],
            recv_sem=g_recv.at[n, o],
            device_id=(leaf_peers[peer], shard),
            device_id_type=MESH,
        )
        copy.start()
        solutions[n, o] = copy

    for n in range(cuts):
        left = residue[n]
        for h in steps[:-1]:
            sums[n, h].wait_recv()
            left = left - along[n, h]
        for i in range(top_each):
            top_out[me * top_each + i, n * half : (n + 1) * half] = dot3(
                split(left[i]), gram[i], 1, 0
            )
        for h in steps[:-1]:
            pass_on(n, 0, 2 * h, 2 * h)
        pass_on(n, 0, 1, 1)
    for n in range(cuts):
        for h in reversed(steps[:-1]):
            solutions[n, 2 * h].wait_recv()
            pass_on(n, 2 * h, 2 * h + 1, 1)
    for copy in [*row_copies.values(), *forwards, *cross.values(), *sums.values()]:
        copy.wait_send()
    for n in range(cuts):
        for h in reversed(steps):
            solutions[n, 2 * h + 1].wait_recv()
        dates_here = slice(n * half, (n + 1) * half)
        for l in range(local):
            own = weight[l][0] * top_out[0, dates_here]
            for p in range(1, tops_all):
                own = own + weight[l][p] * top_out[p, dates_here]
            lifted = dot3(split(own), (wide[0, l], wide[1, l]), 1, 0)
            leaf_out[l, dates_here] = base[l, dates_here] - lifted
    for copy in solutions.values():
        copy.wait_send()


def write_out(leaf_v, top_v, leaf_h, top_h, sems):
    copies = [
        pltpu.make_async_copy(leaf_v, leaf_h, sems.at[0]),
        pltpu.make_async_copy(top_v, top_h, sems.at[1]),
    ]
    for copy in copies:
        copy.start()
    for copy in copies:
        copy.wait()


def fused(
    obs_coef, obs_data, obs_target, leaf_map, leaf_parent, leaf_inv, leaf_off, top_inv, top_rhs
):
    groups, shards = lax.axis_size("leaf"), lax.axis_size("rhs")
    rows = obs_target.shape[0]
    capacity = 2 * rows // groups
    local, width = leaf_inv.shape[0], leaf_inv.shape[1]
    top_count, dates = top_inv.shape[0], obs_data.shape[0]
    top_each = top_count // groups
    coef_rows = obs_coef.shape[0]
    piece = capacity * coef_rows // LANES
    payload = piece + dates // 2 + 8
    pair = groups // 2
    cuts = 2 if dates % 16 == 0 else 1
    half = dates // cuts
    dma = pltpu.SemaphoreType.DMA
    vmem = pl.BlockSpec(memory_space=pltpu.VMEM)
    hbm = pl.BlockSpec(memory_space=pltpu.HBM)
    results = (
        jax.ShapeDtypeStruct((local, dates, width), F32),
        jax.ShapeDtypeStruct((top_count, dates, width), F32),
    )
    solved = pl.pallas_call(
        functools.partial(kernel, groups, shards, capacity),
        out_shape=results,
        in_specs=[hbm] * 9,
        out_specs=(vmem, vmem),
        scratch_shapes=[
            pltpu.VMEM((1, rows), jnp.int32),
            pltpu.VMEM(obs_coef.shape, F32),
            pltpu.VMEM(obs_data.shape, F32),
            pltpu.SMEM(leaf_map.shape, jnp.int32),
            pltpu.SMEM(leaf_parent.shape, jnp.int32),
            pltpu.VMEM(leaf_inv.shape, F32),
            pltpu.VMEM(leaf_off.shape, F32),
            pltpu.VMEM((top_each, width, width), F32),
            pltpu.VMEM((top_each, dates, width), F32),
            pltpu.VMEM((groups, payload, LANES), F32),
            pltpu.VMEM((groups, payload, LANES), F32),
            pltpu.VMEM((shards, groups, piece, LANES), F32),
            pltpu.VMEM((2, local, width, width), BF16),
            pltpu.VMEM((local, dates, width), F32),
            pltpu.VMEM((cuts, top_count, half, width), F32),
            pltpu.VMEM((cuts, groups // 2, top_each, half, width), F32),
            pltpu.VMEM((cuts, groups // 2, top_each, half, width), F32),
            pltpu.VMEM((cuts, groups // 2, top_each, half, width), F32),
            dma((groups,)),
            dma((groups,)),
            dma((shards, pair)),
            dma((shards, pair)),
            dma((cuts, groups // 2)),
            dma((cuts, groups // 2)),
            dma((cuts, groups // 2)),
            dma((cuts, groups // 2)),
            dma((cuts, groups)),
            dma((cuts, groups)),
            dma((9,)),
        ],
        compiler_params=pltpu.CompilerParams(
            collective_id=0, has_side_effects=True, vmem_limit_bytes=24 * 2**20
        ),
    )(
        *(
            pltpu.with_memory_space_constraint(x, pltpu.HBM)
            for x in (
                obs_target.reshape(1, rows), obs_coef, obs_data, leaf_map, leaf_parent,
                leaf_inv, leaf_off, top_inv, top_rhs,
            )
        )
    )
    return pl.pallas_call(
        write_out,
        out_shape=results,
        in_specs=[vmem, vmem],
        out_specs=(hbm, hbm),
        scratch_shapes=[dma((2,))],
        compiler_params=pltpu.CompilerParams(vmem_limit_bytes=4 * 2**20),
    )(*solved)


def plain(
    obs_coef, obs_data, obs_target, leaf_map, leaf_parent, leaf_inv, leaf_off, top_inv, top_rhs
):
    highest = lax.Precision.HIGHEST
    groups = lax.axis_size("leaf")
    device_index = lax.axis_index("leaf")
    local_count = leaf_inv.shape[0]
    block_width = leaf_inv.shape[1]
    top_count = top_inv.shape[0]
    date_cols = obs_data.shape[0]
    rows_here = obs_target.shape[0]
    leaf_total = leaf_map.shape[0]
    capacity = max(2, 2 * rows_here // groups)
    slots_total = groups * capacity
    all_ids = jnp.arange(leaf_total, dtype=jnp.int32)
    id_match = obs_target[:, None] == all_ids[None, :]
    position = jnp.sum(jnp.where(id_match, leaf_map[None, :], 0), axis=1)
    owner_dev = position // local_count
    member = position % local_count
    row_ids = jnp.arange(rows_here, dtype=jnp.int32)
    earlier = (owner_dev[:, None] == owner_dev[None, :]) & (row_ids[:, None] > row_ids[None, :])
    queue_rank = jnp.sum(earlier.astype(jnp.int32), axis=1)
    target_slot = owner_dev * capacity + queue_rank
    slot_mark = (member + 1).astype(jnp.float32)[None, :]
    fields = jnp.concatenate([obs_coef, obs_data, slot_mark], axis=0)
    placed = jnp.zeros((fields.shape[0], slots_total), F32).at[:, target_slot].set(fields)
    received = lax.all_to_all(placed, "leaf", split_axis=1, concat_axis=1, tiled=True)
    part_coef = received[: obs_coef.shape[0]]
    recv_data = received[obs_coef.shape[0] : -1]
    recv_mark = received[-1:]
    recv_coef = lax.all_gather(part_coef, "rhs", axis=0, tiled=True)
    slot_values = (jnp.arange(local_count, dtype=jnp.int32) + 1).astype(jnp.float32)
    chosen = (recv_mark[0][None, :] == slot_values[:, None]).astype(jnp.float32)
    spread = (recv_data[None, :, :] * chosen[:, None, :]).reshape(
        local_count * date_cols, slots_total
    )
    leaf_rhs = lax.dot_general(
        spread, recv_coef, (((1,), (1,)), ((), ())), precision=highest
    ).reshape(local_count, date_cols, block_width)
    solved = jnp.einsum("ltc,ldc->ltd", leaf_rhs, leaf_inv, precision=highest)
    update = jnp.einsum("ltd,lcd->ltc", solved, leaf_off, precision=highest)
    positions_here = device_index * local_count + jnp.arange(local_count, dtype=jnp.int32)
    holder_match = leaf_map[None, :] == positions_here[:, None]
    parent_here = jnp.sum(jnp.where(holder_match, leaf_parent[None, :], 0), axis=1)
    to_top = (parent_here[:, None] == jnp.arange(top_count, dtype=jnp.int32)[None, :]).astype(
        jnp.float32
    )
    contrib = jnp.einsum("lp,ltc->ptc", to_top, update, precision=highest)
    flat_terms = contrib.reshape(top_count * date_cols, block_width)
    top_total = lax.psum(flat_terms, "leaf").reshape(top_count, date_cols, block_width)
    residue = top_rhs - top_total
    top_solved = jnp.einsum("ptc,pdc->ptd", residue, top_inv, precision=highest)
    top_solution = jnp.einsum("ptd,pdc->ptc", top_solved, top_inv, precision=highest)
    from_top = jnp.einsum("lp,ptc->ltc", to_top, top_solution, precision=highest)
    lifted = jnp.einsum("ltc,lcd->ltd", from_top, leaf_off, precision=highest)
    leaf_solution = jnp.einsum("ltc,lcd->ltd", solved - lifted, leaf_inv, precision=highest)
    return (leaf_solution, top_solution)


def body(*args):
    obs_coef, obs_data, obs_target = args[:3]
    groups = lax.axis_size("leaf")
    coef_rows, rows = obs_coef.shape
    dates = obs_data.shape[0]
    fits = (
        args[7].shape[0] % groups == 0
        and groups % 4 == 0
        and groups & (groups - 1) == 0
        and rows % LANES == 0
        and (2 * rows) % groups == 0
        and LANES % coef_rows == 0
        and (2 * rows // groups) % (8 * (LANES // coef_rows)) == 0
        and coef_rows % 8 == 0
        and dates % 16 == 0
        and 2 * (2 * rows // groups) == LANES
        and args[5].shape[1] == LANES
    )
    return fused(*args) if fits else plain(*args)


def solution(mesh):
    return jax.shard_map(
        body,
        mesh=mesh,
        in_specs=(
            P("rhs", "leaf"),
            P("rhs", "leaf"),
            P("leaf"),
            P(),
            P(),
            P("leaf", None, None),
            P("leaf", None, None),
            P(),
            P(None, "rhs", None),
        ),
        out_specs=(P("leaf", "rhs", None), P(None, "rhs", None)),
        check_vma=False,
    )
```

```python
import functools

import jax
import jax.numpy as jnp
from jax import lax
from jax.experimental import pallas as pl
from jax.experimental.pallas import tpu as pltpu
from jax.sharding import PartitionSpec as P

F32, BF16 = jnp.float32, jnp.bfloat16
MESH = pl.DeviceIdType.MESH
LANES = 128


def split(x):
    high = x.astype(BF16)
    return high, (x - high.astype(F32)).astype(BF16)


def contract(a, b, ca, cb):
    return lax.dot_general(a, b, (((ca,), (cb,)), ((), ())), preferred_element_type=F32)


def dot3(a, b, ca, cb):
    (ah, al), (bh, bl) = a, b
    return contract(ah, bh, ca, cb) + (contract(ah, bl, ca, cb) + contract(al, bh, ca, cb))


def flipped(index, bits, count):
    out = index
    place = 1
    while place < count:
        if bits & place:
            out = out + place * (1 - 2 * lax.rem(lax.div(index, place), 2))
        place *= 2
    return out


def kernel(
    groups, shards, capacity,
    tgt_h, coef_h, data_h, lmap_h, lpar_h, inv_h, off_h, tinv_h, trhs_h,
    leaf_out, top_out,
    tgt, coef, data, lmap, lpar, inv, off, tinv, trhs,
    send, recv, packed, wide, base, parts, across, joined, along,
    d_send, d_recv, f_send, f_recv, a_send, a_recv, z_send, z_recv, g_send, g_recv, l_sem,
):
    me = lax.axis_index("leaf")
    shard = lax.axis_index("rhs")
    local, width = inv.shape[0], inv.shape[1]
    coef_rows, rows = coef.shape
    dates = data.shape[0]
    top_each = tinv.shape[0]
    total = lmap.shape[0]
    fold = LANES // coef_rows
    piece = capacity // fold
    pair = f_send.shape[1]
    cuts, tops_all, half = parts.shape[0], parts.shape[1], parts.shape[2]
    per = groups // pair
    leaf_peers = [flipped(me, o, groups) for o in range(groups)]
    far_first = sorted(range(1, groups), key=lambda o: (-(o.bit_length()), o))
    order = [0]
    for o in range(groups // 2):
        order += [groups // 2 + o] + ([o + 1] if o + 1 < groups // 2 else [])
    rhs_peers = [flipped(shard, o, shards) for o in range(shards)]

    barrier = pltpu.get_barrier_semaphore()
    for o in range(1, groups):
        pl.semaphore_signal(barrier, inc=1, device_id=(leaf_peers[o], shard), device_id_type=MESH)
    for o in (1, 2):
        pl.semaphore_signal(barrier, inc=1, device_id=(me, rhs_peers[o]), device_id_type=MESH)
    tops = pl.ds(me * top_each, top_each)
    loads = []
    for i, (src, dst) in enumerate(
        [
            (tgt_h, tgt),
            (lmap_h, lmap),
            (coef_h, coef),
            (data_h, data),
            (lpar_h, lpar),
            (inv_h, inv),
            (off_h, off),
            (tinv_h.at[tops], tinv),
            (trhs_h.at[tops], trhs),
        ]
    ):
        copy = pltpu.make_async_copy(src, dst, l_sem.at[i])
        copy.start()
        loads.append(copy)
    loads[0].wait()
    loads[1].wait()

    target = tgt[...]
    position = jnp.zeros_like(target)
    for i in range(total):
        position = jnp.where(target == i, lmap[i], position)
    place = lax.broadcasted_iota(jnp.int32, (groups, rows), 0)
    first = jnp.zeros_like(place)
    for o in range(groups):
        first = jnp.where(place == o, leaf_peers[o] * local, first)
    member = jnp.broadcast_to(position, (groups, rows)) - first
    owned = (member >= 0) & (member < local)
    hot = jnp.where(owned, 1.0, 0.0)
    before = (
        lax.broadcasted_iota(jnp.int32, (rows, rows), 0)
        < lax.broadcasted_iota(jnp.int32, (rows, rows), 1)
    )
    rank = contract(hot.astype(BF16), jnp.where(before, 1.0, 0.0).astype(BF16), 1, 0)
    slot = jnp.where(owned, rank.astype(jnp.int32), -1)
    mark = jnp.sum(hot * (member + 1).astype(F32), axis=0, keepdims=True)
    slot_ids = lax.broadcasted_iota(jnp.int32, (capacity, rows), 0)
    loads[2].wait()
    loads[3].wait()
    gap = lambda n: [jnp.zeros((n, rows), F32)] if n else []
    coef_fields = split(
        jnp.concatenate(
            [
                jnp.concatenate(
                    gap(q * coef_rows) + [coef[...]] + gap((fold - 1 - q) * coef_rows), axis=0
                )
                for q in range(fold)
            ],
            axis=1,
        )
    )
    marks = jnp.broadcast_to(mark, (8, rows))
    date_fields = split(
        jnp.concatenate(
            [
                jnp.concatenate([data[: dates // 2], marks], axis=0),
                jnp.concatenate([data[dates // 2 :], marks], axis=0),
            ],
            axis=1,
        )
    )

    def place_rows(o, i):
        chosen = jnp.where(slot_ids == slot[o : o + 1, :], 1.0, 0.0)
        folded = jnp.concatenate(
            [chosen[q * piece : (q + 1) * piece] for q in range(fold)], axis=1
        ).astype(BF16)
        none = jnp.zeros_like(chosen)
        doubled = jnp.concatenate(
            [
                jnp.concatenate([chosen, none], axis=1),
                jnp.concatenate([none, chosen], axis=1),
            ],
            axis=0,
        ).astype(BF16)
        send[i, :piece] = contract(folded, coef_fields[0], 1, 1) + contract(
            folded, coef_fields[1], 1, 1
        )
        send[i, piece:] = contract(date_fields[0], doubled, 1, 1) + contract(
            date_fields[1], doubled, 1, 1
        )

    pl.semaphore_wait(barrier, groups - 1 + 2)
    row_copies = {}
    for i in range(1, groups):
        o = order[i]
        place_rows(o, i)
        copy = pltpu.make_async_remote_copy(
            src_ref=send.at[i],
            dst_ref=recv.at[i],
            send_sem=d_send.at[i],
            recv_sem=d_recv.at[i],
            device_id=(leaf_peers[o], shard),
            device_id_type=MESH,
        )
        copy.start()
        row_copies[i] = copy
    place_rows(0, 0)
    recv[0] = send[0]

    for copy in loads[4:]:
        copy.wait()
    for l in range(local):
        high, low = split(dot3(split(off[l]), split(inv[l]), 1, 0))
        wide[0, l] = high
        wide[1, l] = low
    gram = []
    for i in range(top_each):
        block = split(tinv[i])
        gram.append(split(dot3(block, block, 0, 0)))
    up = []
    for l in range(local):
        found = jnp.int32(0)
        for i in range(total):
            found = jnp.where(lmap[i] == me * local + l, lpar[i], found)
        up.append(found)

    crossed, beside, relayed = [], [], []

    def hand_on(src, which, peer, g):
        copy = pltpu.make_async_remote_copy(
            src_ref=src,
            dst_ref=packed.at[rhs_peers[which], pl.ds(g * per, per)],
            send_sem=f_send.at[peer + which, g],
            recv_sem=f_recv.at[peer + which, g],
            device_id=(me, rhs_peers[peer]),
            device_id_type=MESH,
        )
        copy.start()
        return copy

    def relay(g):
        crossed[g].wait_recv()
        span = pl.ds(g * per, per)
        relayed.append(hand_on(packed.at[rhs_peers[2], span], 2, 1, g))

    for g in range(pair):
        for i in range(g * per, (g + 1) * per):
            if i > 0:
                row_copies[i].wait_recv()
            packed[shard, i] = recv[i, :piece]
        landed = recv.at[pl.ds(g * per, per), pl.ds(0, piece)]
        crossed.append(hand_on(landed, 0, 2, g))
        beside.append(hand_on(landed, 0, 1, g))
        if g > 0:
            relay(g - 1)
    relay(pair - 1)
    forwards = [copy for both in zip(beside, relayed) for copy in both]
    ready = len(forwards) // 2
    span = groups // 2
    big_group = lax.broadcasted_iota(jnp.int32, (span * piece, LANES), 1) // coef_rows
    rhs_all = None
    first_half = lax.broadcasted_iota(jnp.int32, (recv.shape[1] - piece, LANES), 1) < capacity
    for part in range(2):
        here = slice(part * span, (part + 1) * span)
        series, marked = [], []
        for i in range(part * span, (part + 1) * span, 2):
            one, two = recv[i, piece:], recv[i + 1, piece:]
            early = jnp.where(first_half, one, pltpu.roll(two, capacity, 1))
            late = jnp.where(first_half, pltpu.roll(one, capacity, 1), two)
            series.append(jnp.concatenate([early[: dates // 2], late[: dates // 2]], axis=0))
            marked.append(early[dates // 2 : dates // 2 + 1])
        series = jnp.concatenate(series, axis=1)
        marked = jnp.concatenate(marked, axis=1)
        spread = split(
            jnp.concatenate(
                [jnp.where(marked == float(l + 1), series, 0.0) for l in range(local)], axis=0
            )
        )
        for copy in forwards[part * ready : (part + 1) * ready]:
            copy.wait_recv()
        packs = [packed[s, here].reshape(span * piece, LANES) for s in range(shards)]
        pieces = []
        for q in range(fold):
            out = None
            for s in range(shards):
                shift = ((s - q) * coef_rows) % LANES
                moved = pltpu.roll(packs[s], shift, 1) if shift else packs[s]
                out = moved if out is None else jnp.where(big_group == s, moved, out)
            pieces.append(out.reshape(span, 1, piece, LANES))
        coefs = jnp.concatenate(pieces, axis=1).reshape(span * capacity, LANES)
        term = dot3(spread, split(coefs), 1, 0)
        rhs_all = term if rhs_all is None else rhs_all + term
    rhs = [
        [split(rhs_all[l * dates + n : l * dates + n + half]) for l in range(local)]
        for n in range(0, dates, half)
    ]
    steps = [h // 2 for h in far_first if h % 2 == 0] + [0]
    cross, sums, solutions = {}, {}, {}
    weight = [[jnp.where(up[l] == p, 1.0, 0.0) for p in range(tops_all)] for l in range(local)]
    for n in range(cuts):
        updates = [dot3(rhs[n][l], (wide[0, l], wide[1, l]), 1, 1) for l in range(local)]
        for p in range(tops_all):
            acc = weight[0][p] * updates[0]
            for l in range(1, local):
                acc = acc + weight[l][p] * updates[l]
            parts[n, p] = acc
        for h in steps:
            copy = pltpu.make_async_remote_copy(
                src_ref=parts.at[n, pl.ds(leaf_peers[2 * h + 1] * top_each, top_each)],
                dst_ref=across.at[n, h],
                send_sem=a_send.at[n, h],
                recv_sem=a_recv.at[n, h],
                device_id=(leaf_peers[1], shard),
                device_id_type=MESH,
            )
            copy.start()
            cross[n, h] = copy
    residue = []
    for n in range(cuts):
        for h in steps:
            cross[n, h].wait_recv()
            here = parts[n, pl.ds(leaf_peers[2 * h] * top_each, top_each)] + across[n, h]
            if h == 0:
                residue.append(trhs[:, n * half : (n + 1) * half] - here)
                continue
            joined[n, h] = here
            copy = pltpu.make_async_remote_copy(
                src_ref=joined.at[n, h],
                dst_ref=along.at[n, h],
                send_sem=z_send.at[n, h],
                recv_sem=z_recv.at[n, h],
                device_id=(leaf_peers[2 * h], shard),
                device_id_type=MESH,
            )
            copy.start()
            sums[n, h] = copy
    for l in range(local):
        factor = split(inv[l])
        for n in range(cuts):
            solved = split(dot3(rhs[n][l], factor, 1, 1))
            base[l, n * half : (n + 1) * half] = dot3(solved, factor, 1, 0)

    def pass_on(n, h, o, peer):
        block = top_out.at[pl.ds(leaf_peers[h] * top_each, top_each), pl.ds(n * half, half)]
        copy = pltpu.make_async_remote_copy(
            src_ref=block,
            dst_ref=block,
            send_sem=g_send.at[n, o],
            recv_sem=g_recv.at[n, o],
            device_id=(leaf_peers[peer], shard),
            device_id_type=MESH,
        )
        copy.start()
        solutions[n, o] = copy

    for n in range(cuts):
        left = residue[n]
        for h in steps[:-1]:
            sums[n, h].wait_recv()
            left = left - along[n, h]
        for i in range(top_each):
            top_out[me * top_each + i, n * half : (n + 1) * half] = dot3(
                split(left[i]), gram[i], 1, 0
            )
        for h in steps[:-1]:
            pass_on(n, 0, 2 * h, 2 * h)
        pass_on(n, 0, 1, 1)
    for n in range(cuts):
        for h in reversed(steps[:-1]):
            solutions[n, 2 * h].wait_recv()
            pass_on(n, 2 * h, 2 * h + 1, 1)
    for copy in [*row_copies.values(), *crossed, *forwards, *cross.values(), *sums.values()]:
        copy.wait_send()
    for n in range(cuts):
        for h in reversed(steps):
            solutions[n, 2 * h + 1].wait_recv()
        dates_here = slice(n * half, (n + 1) * half)
        for l in range(local):
            own = weight[l][0] * top_out[0, dates_here]
            for p in range(1, tops_all):
                own = own + weight[l][p] * top_out[p, dates_here]
            lifted = dot3(split(own), (wide[0, l], wide[1, l]), 1, 0)
            leaf_out[l, dates_here] = base[l, dates_here] - lifted
    for copy in solutions.values():
        copy.wait_send()


def write_out(leaf_v, top_v, leaf_h, top_h, sems):
    copies = [
        pltpu.make_async_copy(leaf_v, leaf_h, sems.at[0]),
        pltpu.make_async_copy(top_v, top_h, sems.at[1]),
    ]
    for copy in copies:
        copy.start()
    for copy in copies:
        copy.wait()


def fused(
    obs_coef, obs_data, obs_target, leaf_map, leaf_parent, leaf_inv, leaf_off, top_inv, top_rhs
):
    groups, shards = lax.axis_size("leaf"), lax.axis_size("rhs")
    rows = obs_target.shape[0]
    capacity = 2 * rows // groups
    local, width = leaf_inv.shape[0], leaf_inv.shape[1]
    top_count, dates = top_inv.shape[0], obs_data.shape[0]
    top_each = top_count // groups
    coef_rows = obs_coef.shape[0]
    piece = capacity * coef_rows // LANES
    payload = piece + dates // 2 + 8
    pair = groups // 2
    cuts = 2 if dates % 16 == 0 else 1
    half = dates // cuts
    dma = pltpu.SemaphoreType.DMA
    vmem = pl.BlockSpec(memory_space=pltpu.VMEM)
    hbm = pl.BlockSpec(memory_space=pltpu.HBM)
    results = (
        jax.ShapeDtypeStruct((local, dates, width), F32),
        jax.ShapeDtypeStruct((top_count, dates, width), F32),
    )
    solved = pl.pallas_call(
        functools.partial(kernel, groups, shards, capacity),
        out_shape=results,
        in_specs=[hbm] * 9,
        out_specs=(vmem, vmem),
        scratch_shapes=[
            pltpu.VMEM((1, rows), jnp.int32),
            pltpu.VMEM(obs_coef.shape, F32),
            pltpu.VMEM(obs_data.shape, F32),
            pltpu.SMEM(leaf_map.shape, jnp.int32),
            pltpu.SMEM(leaf_parent.shape, jnp.int32),
            pltpu.VMEM(leaf_inv.shape, F32),
            pltpu.VMEM(leaf_off.shape, F32),
            pltpu.VMEM((top_each, width, width), F32),
            pltpu.VMEM((top_each, dates, width), F32),
            pltpu.VMEM((groups, payload, LANES), F32),
            pltpu.VMEM((groups, payload, LANES), F32),
            pltpu.VMEM((shards, groups, piece, LANES), F32),
            pltpu.VMEM((2, local, width, width), BF16),
            pltpu.VMEM((local, dates, width), F32),
            pltpu.VMEM((cuts, top_count, half, width), F32),
            pltpu.VMEM((cuts, groups // 2, top_each, half, width), F32),
            pltpu.VMEM((cuts, groups // 2, top_each, half, width), F32),
            pltpu.VMEM((cuts, groups // 2, top_each, half, width), F32),
            dma((groups,)),
            dma((groups,)),
            dma((shards, pair)),
            dma((shards, pair)),
            dma((cuts, groups // 2)),
            dma((cuts, groups // 2)),
            dma((cuts, groups // 2)),
            dma((cuts, groups // 2)),
            dma((cuts, groups)),
            dma((cuts, groups)),
            dma((9,)),
        ],
        compiler_params=pltpu.CompilerParams(
            collective_id=0, has_side_effects=True, vmem_limit_bytes=24 * 2**20
        ),
    )(
        *(
            pltpu.with_memory_space_constraint(x, pltpu.HBM)
            for x in (
                obs_target.reshape(1, rows), obs_coef, obs_data, leaf_map, leaf_parent,
                leaf_inv, leaf_off, top_inv, top_rhs,
            )
        )
    )
    return pl.pallas_call(
        write_out,
        out_shape=results,
        in_specs=[vmem, vmem],
        out_specs=(hbm, hbm),
        scratch_shapes=[dma((2,))],
        compiler_params=pltpu.CompilerParams(vmem_limit_bytes=4 * 2**20),
    )(*solved)


def plain(
    obs_coef, obs_data, obs_target, leaf_map, leaf_parent, leaf_inv, leaf_off, top_inv, top_rhs
):
    highest = lax.Precision.HIGHEST
    groups = lax.axis_size("leaf")
    device_index = lax.axis_index("leaf")
    local_count = leaf_inv.shape[0]
    block_width = leaf_inv.shape[1]
    top_count = top_inv.shape[0]
    date_cols = obs_data.shape[0]
    rows_here = obs_target.shape[0]
    leaf_total = leaf_map.shape[0]
    capacity = max(2, 2 * rows_here // groups)
    slots_total = groups * capacity
    all_ids = jnp.arange(leaf_total, dtype=jnp.int32)
    id_match = obs_target[:, None] == all_ids[None, :]
    position = jnp.sum(jnp.where(id_match, leaf_map[None, :], 0), axis=1)
    owner_dev = position // local_count
    member = position % local_count
    row_ids = jnp.arange(rows_here, dtype=jnp.int32)
    earlier = (owner_dev[:, None] == owner_dev[None, :]) & (row_ids[:, None] > row_ids[None, :])
    queue_rank = jnp.sum(earlier.astype(jnp.int32), axis=1)
    target_slot = owner_dev * capacity + queue_rank
    slot_mark = (member + 1).astype(jnp.float32)[None, :]
    fields = jnp.concatenate([obs_coef, obs_data, slot_mark], axis=0)
    placed = jnp.zeros((fields.shape[0], slots_total), F32).at[:, target_slot].set(fields)
    received = lax.all_to_all(placed, "leaf", split_axis=1, concat_axis=1, tiled=True)
    part_coef = received[: obs_coef.shape[0]]
    recv_data = received[obs_coef.shape[0] : -1]
    recv_mark = received[-1:]
    recv_coef = lax.all_gather(part_coef, "rhs", axis=0, tiled=True)
    slot_values = (jnp.arange(local_count, dtype=jnp.int32) + 1).astype(jnp.float32)
    chosen = (recv_mark[0][None, :] == slot_values[:, None]).astype(jnp.float32)
    spread = (recv_data[None, :, :] * chosen[:, None, :]).reshape(
        local_count * date_cols, slots_total
    )
    leaf_rhs = lax.dot_general(
        spread, recv_coef, (((1,), (1,)), ((), ())), precision=highest
    ).reshape(local_count, date_cols, block_width)
    solved = jnp.einsum("ltc,ldc->ltd", leaf_rhs, leaf_inv, precision=highest)
    update = jnp.einsum("ltd,lcd->ltc", solved, leaf_off, precision=highest)
    positions_here = device_index * local_count + jnp.arange(local_count, dtype=jnp.int32)
    holder_match = leaf_map[None, :] == positions_here[:, None]
    parent_here = jnp.sum(jnp.where(holder_match, leaf_parent[None, :], 0), axis=1)
    to_top = (parent_here[:, None] == jnp.arange(top_count, dtype=jnp.int32)[None, :]).astype(
        jnp.float32
    )
    contrib = jnp.einsum("lp,ltc->ptc", to_top, update, precision=highest)
    flat_terms = contrib.reshape(top_count * date_cols, block_width)
    top_total = lax.psum(flat_terms, "leaf").reshape(top_count, date_cols, block_width)
    residue = top_rhs - top_total
    top_solved = jnp.einsum("ptc,pdc->ptd", residue, top_inv, precision=highest)
    top_solution = jnp.einsum("ptd,pdc->ptc", top_solved, top_inv, precision=highest)
    from_top = jnp.einsum("lp,ptc->ltc", to_top, top_solution, precision=highest)
    lifted = jnp.einsum("ltc,lcd->ltd", from_top, leaf_off, precision=highest)
    leaf_solution = jnp.einsum("ltc,lcd->ltd", solved - lifted, leaf_inv, precision=highest)
    return (leaf_solution, top_solution)


def body(*args):
    obs_coef, obs_data, obs_target = args[:3]
    groups = lax.axis_size("leaf")
    coef_rows, rows = obs_coef.shape
    dates = obs_data.shape[0]
    fits = (
        args[7].shape[0] % groups == 0
        and groups % 4 == 0
        and lax.axis_size("rhs") == 4
        and groups & (groups - 1) == 0
        and rows % LANES == 0
        and (2 * rows) % groups == 0
        and LANES % coef_rows == 0
        and (2 * rows // groups) % (8 * (LANES // coef_rows)) == 0
        and coef_rows % 8 == 0
        and dates % 16 == 0
        and 2 * (2 * rows // groups) == LANES
        and args[5].shape[1] == LANES
    )
    return fused(*args) if fits else plain(*args)


def solution(mesh):
    return jax.shard_map(
        body,
        mesh=mesh,
        in_specs=(
            P("rhs", "leaf"),
            P("rhs", "leaf"),
            P("leaf"),
            P(),
            P(),
            P("leaf", None, None),
            P("leaf", None, None),
            P(),
            P(None, "rhs", None),
        ),
        out_specs=(P("leaf", "rhs", None), P(None, "rhs", None)),
        check_vma=False,
    )
```

```python
import functools

import jax
import jax.numpy as jnp
from jax import lax
from jax.experimental import pallas as pl
from jax.experimental.pallas import tpu as pltpu
from jax.sharding import PartitionSpec as P

F32, BF16 = jnp.float32, jnp.bfloat16
MESH = pl.DeviceIdType.MESH
LANES = 128


def split(x):
    high = x.astype(BF16)
    return high, (x - high.astype(F32)).astype(BF16)


def contract(a, b, ca, cb):
    return lax.dot_general(a, b, (((ca,), (cb,)), ((), ())), preferred_element_type=F32)


def dot3(a, b, ca, cb):
    (ah, al), (bh, bl) = a, b
    return contract(ah, bh, ca, cb) + (contract(ah, bl, ca, cb) + contract(al, bh, ca, cb))


def flipped(index, bits, count):
    out = index
    place = 1
    while place < count:
        if bits & place:
            out = out + place * (1 - 2 * lax.rem(lax.div(index, place), 2))
        place *= 2
    return out


def kernel(
    groups, shards, capacity,
    tgt_h, coef_h, data_h, lmap_h, lpar_h, inv_h, off_h, tinv_h, trhs_h,
    leaf_out, top_out,
    tgt, coef, data, lmap, lpar, inv, off, tinv, trhs,
    send, recv, packed, wide, base, parts, across, joined, along,
    d_send, d_recv, f_send, f_recv, a_send, a_recv, z_send, z_recv, g_send, g_recv, l_sem,
):
    me = lax.axis_index("leaf")
    shard = lax.axis_index("rhs")
    local, width = inv.shape[0], inv.shape[1]
    coef_rows, rows = coef.shape
    dates = data.shape[0]
    top_each = tinv.shape[0]
    total = lmap.shape[0]
    fold = LANES // coef_rows
    piece = capacity // fold
    pair = f_send.shape[1]
    cuts, tops_all, half = parts.shape[0], parts.shape[1], parts.shape[2]
    per = groups // pair
    leaf_peers = [flipped(me, o, groups) for o in range(groups)]
    far_first = sorted(range(1, groups), key=lambda o: (-(o.bit_length()), o))
    order = [0]
    for o in range(groups // 2):
        order += [groups // 2 + o] + ([o + 1] if o + 1 < groups // 2 else [])
    rhs_peers = [lax.rem(shard + o, shards) for o in range(shards)]

    barrier = pltpu.get_barrier_semaphore()
    for o in range(1, groups):
        pl.semaphore_signal(barrier, inc=1, device_id=(leaf_peers[o], shard), device_id_type=MESH)
    for o in range(1, shards):
        pl.semaphore_signal(barrier, inc=1, device_id=(me, rhs_peers[o]), device_id_type=MESH)
    tops = pl.ds(me * top_each, top_each)
    loads = []
    for i, (src, dst) in enumerate(
        [
            (tgt_h, tgt),
            (lmap_h, lmap),
            (coef_h, coef),
            (data_h, data),
            (lpar_h, lpar),
            (inv_h, inv),
            (off_h, off),
            (tinv_h.at[tops], tinv),
            (trhs_h.at[tops], trhs),
        ]
    ):
        copy = pltpu.make_async_copy(src, dst, l_sem.at[i])
        copy.start()
        loads.append(copy)
    loads[0].wait()
    loads[1].wait()

    target = tgt[...]
    position = jnp.zeros_like(target)
    for i in range(total):
        position = jnp.where(target == i, lmap[i], position)
    place = lax.broadcasted_iota(jnp.int32, (groups, rows), 0)
    first = jnp.zeros_like(place)
    for o in range(groups):
        first = jnp.where(place == o, leaf_peers[o] * local, first)
    member = jnp.broadcast_to(position, (groups, rows)) - first
    owned = (member >= 0) & (member < local)
    hot = jnp.where(owned, 1.0, 0.0)
    before = (
        lax.broadcasted_iota(jnp.int32, (rows, rows), 0)
        < lax.broadcasted_iota(jnp.int32, (rows, rows), 1)
    )
    rank = contract(hot.astype(BF16), jnp.where(before, 1.0, 0.0).astype(BF16), 1, 0)
    slot = jnp.where(owned, rank.astype(jnp.int32), -1)
    mark = jnp.sum(hot * (member + 1).astype(F32), axis=0, keepdims=True)
    slot_ids = lax.broadcasted_iota(jnp.int32, (capacity, rows), 0)
    loads[2].wait()
    loads[3].wait()
    gap = lambda n: [jnp.zeros((n, rows), F32)] if n else []
    coef_fields = split(
        jnp.concatenate(
            [
                jnp.concatenate(
                    gap(q * coef_rows) + [coef[...]] + gap((fold - 1 - q) * coef_rows), axis=0
                )
                for q in range(fold)
            ],
            axis=1,
        )
    )
    marks = jnp.broadcast_to(mark, (8, rows))
    date_fields = split(
        jnp.concatenate(
            [
                jnp.concatenate([data[: dates // 2], marks], axis=0),
                jnp.concatenate([data[dates // 2 :], marks], axis=0),
            ],
            axis=1,
        )
    )

    def place_rows(o, i):
        chosen = jnp.where(slot_ids == slot[o : o + 1, :], 1.0, 0.0)
        folded = jnp.concatenate(
            [chosen[q * piece : (q + 1) * piece] for q in range(fold)], axis=1
        ).astype(BF16)
        none = jnp.zeros_like(chosen)
        doubled = jnp.concatenate(
            [
                jnp.concatenate([chosen, none], axis=1),
                jnp.concatenate([none, chosen], axis=1),
            ],
            axis=0,
        ).astype(BF16)
        send[i, :piece] = contract(folded, coef_fields[0], 1, 1) + contract(
            folded, coef_fields[1], 1, 1
        )
        send[i, piece:] = contract(date_fields[0], doubled, 1, 1) + contract(
            date_fields[1], doubled, 1, 1
        )

    pl.semaphore_wait(barrier, groups - 1 + shards - 1)
    row_copies = {}
    for i in range(1, groups):
        o = order[i]
        place_rows(o, i)
        copy = pltpu.make_async_remote_copy(
            src_ref=send.at[i],
            dst_ref=recv.at[i],
            send_sem=d_send.at[i],
            recv_sem=d_recv.at[i],
            device_id=(leaf_peers[o], shard),
            device_id_type=MESH,
        )
        copy.start()
        row_copies[i] = copy
    place_rows(0, 0)
    recv[0] = send[0]

    for copy in loads[4:]:
        copy.wait()
    for l in range(local):
        high, low = split(dot3(split(off[l]), split(inv[l]), 1, 0))
        wide[0, l] = high
        wide[1, l] = low
    gram = []
    for i in range(top_each):
        block = split(tinv[i])
        gram.append(split(dot3(block, block, 0, 0)))
    up = []
    for l in range(local):
        found = jnp.int32(0)
        for i in range(total):
            found = jnp.where(lmap[i] == me * local + l, lpar[i], found)
        up.append(found)

    forwards = []
    for g in range(pair):
        for i in range(g * per, (g + 1) * per):
            if i > 0:
                row_copies[i].wait_recv()
            packed[shard, i] = recv[i, :piece]
        span = pl.ds(g * per, per)
        for o in range(1, shards):
            copy = pltpu.make_async_remote_copy(
                src_ref=recv.at[span, pl.ds(0, piece)],
                dst_ref=packed.at[shard, span],
                send_sem=f_send.at[o, g],
                recv_sem=f_recv.at[o, g],
                device_id=(me, rhs_peers[o]),
                device_id_type=MESH,
            )
            copy.start()
            forwards.append(copy)
    ready = len(forwards) // 2
    span = groups // 2
    big_group = lax.broadcasted_iota(jnp.int32, (span * piece, LANES), 1) // coef_rows
    rhs_all = None
    first_half = lax.broadcasted_iota(jnp.int32, (recv.shape[1] - piece, LANES), 1) < capacity
    for part in range(2):
        here = slice(part * span, (part + 1) * span)
        series, marked = [], []
        for i in range(part * span, (part + 1) * span, 2):
            one, two = recv[i, piece:], recv[i + 1, piece:]
            early = jnp.where(first_half, one, pltpu.roll(two, capacity, 1))
            late = jnp.where(first_half, pltpu.roll(one, capacity, 1), two)
            series.append(jnp.concatenate([early[: dates // 2], late[: dates // 2]], axis=0))
            marked.append(early[dates // 2 : dates // 2 + 1])
        series = jnp.concatenate(series, axis=1)
        marked = jnp.concatenate(marked, axis=1)
        spread = split(
            jnp.concatenate(
                [jnp.where(marked == float(l + 1), series, 0.0) for l in range(local)], axis=0
            )
        )
        for copy in forwards[part * ready : (part + 1) * ready]:
            copy.wait_recv()
        packs = [packed[s, here].reshape(span * piece, LANES) for s in range(shards)]
        pieces = []
        for q in range(fold):
            out = None
            for s in range(shards):
                shift = ((s - q) * coef_rows) % LANES
                moved = pltpu.roll(packs[s], shift, 1) if shift else packs[s]
                out = moved if out is None else jnp.where(big_group == s, moved, out)
            pieces.append(out.reshape(span, 1, piece, LANES))
        coefs = jnp.concatenate(pieces, axis=1).reshape(span * capacity, LANES)
        term = dot3(spread, split(coefs), 1, 0)
        rhs_all = term if rhs_all is None else rhs_all + term
    rhs = [
        [split(rhs_all[l * dates + n : l * dates + n + half]) for l in range(local)]
        for n in range(0, dates, half)
    ]
    steps = [h // 2 for h in far_first if h % 2 == 0] + [0]
    cross, sums, solutions = {}, {}, {}
    weight = [[jnp.where(up[l] == p, 1.0, 0.0) for p in range(tops_all)] for l in range(local)]
    for n in range(cuts):
        updates = [dot3(rhs[n][l], (wide[0, l], wide[1, l]), 1, 1) for l in range(local)]
        for p in range(tops_all):
            acc = weight[0][p] * updates[0]
            for l in range(1, local):
                acc = acc + weight[l][p] * updates[l]
            parts[n, p] = acc
        for h in steps:
            copy = pltpu.make_async_remote_copy(
                src_ref=parts.at[n, pl.ds(leaf_peers[2 * h + 1] * top_each, top_each)],
                dst_ref=across.at[n, h],
                send_sem=a_send.at[n, h],
                recv_sem=a_recv.at[n, h],
                device_id=(leaf_peers[1], shard),
                device_id_type=MESH,
            )
            copy.start()
            cross[n, h] = copy
    residue = []
    for n in range(cuts):
        for h in steps:
            cross[n, h].wait_recv()
            here = parts[n, pl.ds(leaf_peers[2 * h] * top_each, top_each)] + across[n, h]
            if h == 0:
                residue.append(trhs[:, n * half : (n + 1) * half] - here)
                continue
            joined[n, h] = here
            copy = pltpu.make_async_remote_copy(
                src_ref=joined.at[n, h],
                dst_ref=along.at[n, h],
                send_sem=z_send.at[n, h],
                recv_sem=z_recv.at[n, h],
                device_id=(leaf_peers[2 * h], shard),
                device_id_type=MESH,
            )
            copy.start()
            sums[n, h] = copy
    for l in range(local):
        factor = split(inv[l])
        for n in range(cuts):
            solved = split(dot3(rhs[n][l], factor, 1, 1))
            base[l, n * half : (n + 1) * half] = dot3(solved, factor, 1, 0)

    def pass_on(n, h, o, peer):
        block = top_out.at[pl.ds(leaf_peers[h] * top_each, top_each), pl.ds(n * half, half)]
        copy = pltpu.make_async_remote_copy(
            src_ref=block,
            dst_ref=block,
            send_sem=g_send.at[n, o],
            recv_sem=g_recv.at[n, o],
            device_id=(leaf_peers[peer], shard),
            device_id_type=MESH,
        )
        copy.start()
        solutions[n, o] = copy

    for n in range(cuts):
        left = residue[n]
        for h in steps[:-1]:
            sums[n, h].wait_recv()
            left = left - along[n, h]
        for i in range(top_each):
            top_out[me * top_each + i, n * half : (n + 1) * half] = dot3(
                split(left[i]), gram[i], 1, 0
            )
        for h in steps[:-1]:
            pass_on(n, 0, 2 * h, 2 * h)
        pass_on(n, 0, 1, 1)
    for n in range(cuts):
        for h in reversed(steps[:-1]):
            solutions[n, 2 * h].wait_recv()
            pass_on(n, 2 * h, 2 * h + 1, 1)
    for copy in [*row_copies.values(), *forwards, *cross.values(), *sums.values()]:
        copy.wait_send()
    for n in range(cuts):
        for h in reversed(steps):
            solutions[n, 2 * h + 1].wait_recv()
        dates_here = slice(n * half, (n + 1) * half)
        for l in range(local):
            own = weight[l][0] * top_out[0, dates_here]
            for p in range(1, tops_all):
                own = own + weight[l][p] * top_out[p, dates_here]
            lifted = dot3(split(own), (wide[0, l], wide[1, l]), 1, 0)
            leaf_out[l, dates_here] = base[l, dates_here] - lifted
    for copy in solutions.values():
        copy.wait_send()


def write_out(leaf_v, top_v, leaf_h, top_h, sems):
    copies = [
        pltpu.make_async_copy(leaf_v, leaf_h, sems.at[0]),
        pltpu.make_async_copy(top_v, top_h, sems.at[1]),
    ]
    for copy in copies:
        copy.start()
    for copy in copies:
        copy.wait()


def fused(
    obs_coef, obs_data, obs_target, leaf_map, leaf_parent, leaf_inv, leaf_off, top_inv, top_rhs
):
    groups, shards = lax.axis_size("leaf"), lax.axis_size("rhs")
    rows = obs_target.shape[0]
    capacity = 2 * rows // groups
    local, width = leaf_inv.shape[0], leaf_inv.shape[1]
    top_count, dates = top_inv.shape[0], obs_data.shape[0]
    top_each = top_count // groups
    coef_rows = obs_coef.shape[0]
    piece = capacity * coef_rows // LANES
    payload = piece + dates // 2 + 8
    pair = 2
    cuts = 1
    half = dates // cuts
    dma = pltpu.SemaphoreType.DMA
    vmem = pl.BlockSpec(memory_space=pltpu.VMEM)
    hbm = pl.BlockSpec(memory_space=pltpu.HBM)
    results = (
        jax.ShapeDtypeStruct((local, dates, width), F32),
        jax.ShapeDtypeStruct((top_count, dates, width), F32),
    )
    solved = pl.pallas_call(
        functools.partial(kernel, groups, shards, capacity),
        out_shape=results,
        in_specs=[hbm] * 9,
        out_specs=(vmem, vmem),
        scratch_shapes=[
            pltpu.VMEM((1, rows), jnp.int32),
            pltpu.VMEM(obs_coef.shape, F32),
            pltpu.VMEM(obs_data.shape, F32),
            pltpu.SMEM(leaf_map.shape, jnp.int32),
            pltpu.SMEM(leaf_parent.shape, jnp.int32),
            pltpu.VMEM(leaf_inv.shape, F32),
            pltpu.VMEM(leaf_off.shape, F32),
            pltpu.VMEM((top_each, width, width), F32),
            pltpu.VMEM((top_each, dates, width), F32),
            pltpu.VMEM((groups, payload, LANES), F32),
            pltpu.VMEM((groups, payload, LANES), F32),
            pltpu.VMEM((shards, groups, piece, LANES), F32),
            pltpu.VMEM((2, local, width, width), BF16),
            pltpu.VMEM((local, dates, width), F32),
            pltpu.VMEM((cuts, top_count, half, width), F32),
            pltpu.VMEM((cuts, groups // 2, top_each, half, width), F32),
            pltpu.VMEM((cuts, groups // 2, top_each, half, width), F32),
            pltpu.VMEM((cuts, groups // 2, top_each, half, width), F32),
            dma((groups,)),
            dma((groups,)),
            dma((shards, pair)),
            dma((shards, pair)),
            dma((cuts, groups // 2)),
            dma((cuts, groups // 2)),
            dma((cuts, groups // 2)),
            dma((cuts, groups // 2)),
            dma((cuts, groups)),
            dma((cuts, groups)),
            dma((9,)),
        ],
        compiler_params=pltpu.CompilerParams(
            collective_id=0, has_side_effects=True, vmem_limit_bytes=24 * 2**20
        ),
    )(
        *(
            pltpu.with_memory_space_constraint(x, pltpu.HBM)
            for x in (
                obs_target.reshape(1, rows), obs_coef, obs_data, leaf_map, leaf_parent,
                leaf_inv, leaf_off, top_inv, top_rhs,
            )
        )
    )
    return pl.pallas_call(
        write_out,
        out_shape=results,
        in_specs=[vmem, vmem],
        out_specs=(hbm, hbm),
        scratch_shapes=[dma((2,))],
        compiler_params=pltpu.CompilerParams(vmem_limit_bytes=4 * 2**20),
    )(*solved)


def plain(
    obs_coef, obs_data, obs_target, leaf_map, leaf_parent, leaf_inv, leaf_off, top_inv, top_rhs
):
    highest = lax.Precision.HIGHEST
    groups = lax.axis_size("leaf")
    device_index = lax.axis_index("leaf")
    local_count = leaf_inv.shape[0]
    block_width = leaf_inv.shape[1]
    top_count = top_inv.shape[0]
    date_cols = obs_data.shape[0]
    rows_here = obs_target.shape[0]
    leaf_total = leaf_map.shape[0]
    capacity = max(2, 2 * rows_here // groups)
    slots_total = groups * capacity
    all_ids = jnp.arange(leaf_total, dtype=jnp.int32)
    id_match = obs_target[:, None] == all_ids[None, :]
    position = jnp.sum(jnp.where(id_match, leaf_map[None, :], 0), axis=1)
    owner_dev = position // local_count
    member = position % local_count
    row_ids = jnp.arange(rows_here, dtype=jnp.int32)
    earlier = (owner_dev[:, None] == owner_dev[None, :]) & (row_ids[:, None] > row_ids[None, :])
    queue_rank = jnp.sum(earlier.astype(jnp.int32), axis=1)
    target_slot = owner_dev * capacity + queue_rank
    slot_mark = (member + 1).astype(jnp.float32)[None, :]
    fields = jnp.concatenate([obs_coef, obs_data, slot_mark], axis=0)
    placed = jnp.zeros((fields.shape[0], slots_total), F32).at[:, target_slot].set(fields)
    received = lax.all_to_all(placed, "leaf", split_axis=1, concat_axis=1, tiled=True)
    part_coef = received[: obs_coef.shape[0]]
    recv_data = received[obs_coef.shape[0] : -1]
    recv_mark = received[-1:]
    recv_coef = lax.all_gather(part_coef, "rhs", axis=0, tiled=True)
    slot_values = (jnp.arange(local_count, dtype=jnp.int32) + 1).astype(jnp.float32)
    chosen = (recv_mark[0][None, :] == slot_values[:, None]).astype(jnp.float32)
    spread = (recv_data[None, :, :] * chosen[:, None, :]).reshape(
        local_count * date_cols, slots_total
    )
    leaf_rhs = lax.dot_general(
        spread, recv_coef, (((1,), (1,)), ((), ())), precision=highest
    ).reshape(local_count, date_cols, block_width)
    solved = jnp.einsum("ltc,ldc->ltd", leaf_rhs, leaf_inv, precision=highest)
    update = jnp.einsum("ltd,lcd->ltc", solved, leaf_off, precision=highest)
    positions_here = device_index * local_count + jnp.arange(local_count, dtype=jnp.int32)
    holder_match = leaf_map[None, :] == positions_here[:, None]
    parent_here = jnp.sum(jnp.where(holder_match, leaf_parent[None, :], 0), axis=1)
    to_top = (parent_here[:, None] == jnp.arange(top_count, dtype=jnp.int32)[None, :]).astype(
        jnp.float32
    )
    contrib = jnp.einsum("lp,ltc->ptc", to_top, update, precision=highest)
    flat_terms = contrib.reshape(top_count * date_cols, block_width)
    top_total = lax.psum(flat_terms, "leaf").reshape(top_count, date_cols, block_width)
    residue = top_rhs - top_total
    top_solved = jnp.einsum("ptc,pdc->ptd", residue, top_inv, precision=highest)
    top_solution = jnp.einsum("ptd,pdc->ptc", top_solved, top_inv, precision=highest)
    from_top = jnp.einsum("lp,ptc->ltc", to_top, top_solution, precision=highest)
    lifted = jnp.einsum("ltc,lcd->ltd", from_top, leaf_off, precision=highest)
    leaf_solution = jnp.einsum("ltc,lcd->ltd", solved - lifted, leaf_inv, precision=highest)
    return (leaf_solution, top_solution)


def body(*args):
    obs_coef, obs_data, obs_target = args[:3]
    groups = lax.axis_size("leaf")
    coef_rows, rows = obs_coef.shape
    dates = obs_data.shape[0]
    fits = (
        args[7].shape[0] % groups == 0
        and groups % 4 == 0
        and groups & (groups - 1) == 0
        and rows % LANES == 0
        and (2 * rows) % groups == 0
        and LANES % coef_rows == 0
        and (2 * rows // groups) % (8 * (LANES // coef_rows)) == 0
        and coef_rows % 8 == 0
        and dates % 16 == 0
        and 2 * (2 * rows // groups) == LANES
        and args[5].shape[1] == LANES
    )
    return fused(*args) if fits else plain(*args)


def solution(mesh):
    return jax.shard_map(
        body,
        mesh=mesh,
        in_specs=(
            P("rhs", "leaf"),
            P("rhs", "leaf"),
            P("leaf"),
            P(),
            P(),
            P("leaf", None, None),
            P("leaf", None, None),
            P(),
            P(None, "rhs", None),
        ),
        out_specs=(P("leaf", "rhs", None), P(None, "rhs", None)),
        check_vma=False,
    )
```

```python
import functools

import jax
import jax.numpy as jnp
from jax import lax
from jax.experimental import pallas as pl
from jax.experimental.pallas import tpu as pltpu
from jax.sharding import PartitionSpec as P

F32, BF16 = jnp.float32, jnp.bfloat16
MESH = pl.DeviceIdType.MESH
LANES = 128


def split(x):
    high = x.astype(BF16)
    return high, (x - high.astype(F32)).astype(BF16)


def contract(a, b, ca, cb):
    return lax.dot_general(a, b, (((ca,), (cb,)), ((), ())), preferred_element_type=F32)


def dot3(a, b, ca, cb):
    (ah, al), (bh, bl) = a, b
    return contract(ah, bh, ca, cb) + (contract(ah, bl, ca, cb) + contract(al, bh, ca, cb))


def flipped(index, bits, count):
    out = index
    place = 1
    while place < count:
        if bits & place:
            out = out + place * (1 - 2 * lax.rem(lax.div(index, place), 2))
        place *= 2
    return out


def kernel(
    groups, shards, capacity,
    tgt_h, coef_h, data_h, lmap_h, lpar_h, inv_h, off_h, tinv_h, trhs_h,
    leaf_out, top_out,
    tgt, coef, data, lmap, lpar, inv, off, tinv, trhs,
    send, recv, packed, wide, base, parts, across, joined, along,
    d_send, d_recv, f_send, f_recv, a_send, a_recv, z_send, z_recv, g_send, g_recv, l_sem,
):
    me = lax.axis_index("leaf")
    shard = lax.axis_index("rhs")
    local, width = inv.shape[0], inv.shape[1]
    coef_rows, rows = coef.shape
    dates = data.shape[0]
    top_each = tinv.shape[0]
    total = lmap.shape[0]
    fold = LANES // coef_rows
    piece = capacity // fold
    pair = f_send.shape[1]
    cuts, tops_all, half = parts.shape[0], parts.shape[1], parts.shape[2]
    per = groups // pair
    leaf_peers = [flipped(me, o, groups) for o in range(groups)]
    far_first = sorted(range(1, groups), key=lambda o: (-(o.bit_length()), o))
    rhs_peers = [lax.rem(shard + o, shards) for o in range(shards)]

    barrier = pltpu.get_barrier_semaphore()
    for o in range(1, groups):
        pl.semaphore_signal(barrier, inc=1, device_id=(leaf_peers[o], shard), device_id_type=MESH)
    for o in range(1, shards):
        pl.semaphore_signal(barrier, inc=1, device_id=(me, rhs_peers[o]), device_id_type=MESH)
    tops = pl.ds(me * top_each, top_each)
    loads = []
    for i, (src, dst) in enumerate(
        [
            (tgt_h, tgt),
            (lmap_h, lmap),
            (coef_h, coef),
            (data_h, data),
            (lpar_h, lpar),
            (inv_h, inv),
            (off_h, off),
            (tinv_h.at[tops], tinv),
            (trhs_h.at[tops], trhs),
        ]
    ):
        copy = pltpu.make_async_copy(src, dst, l_sem.at[i])
        copy.start()
        loads.append(copy)
    loads[0].wait()
    loads[1].wait()

    target = tgt[...]
    position = jnp.zeros_like(target)
    for i in range(total):
        position = jnp.where(target == i, lmap[i], position)
    place = lax.broadcasted_iota(jnp.int32, (groups, rows), 0)
    first = jnp.zeros_like(place)
    for o in range(groups):
        first = jnp.where(place == o, leaf_peers[o] * local, first)
    member = jnp.broadcast_to(position, (groups, rows)) - first
    owned = (member >= 0) & (member < local)
    hot = jnp.where(owned, 1.0, 0.0)
    before = (
        lax.broadcasted_iota(jnp.int32, (rows, rows), 0)
        < lax.broadcasted_iota(jnp.int32, (rows, rows), 1)
    )
    rank = contract(hot.astype(BF16), jnp.where(before, 1.0, 0.0).astype(BF16), 1, 0)
    slot = jnp.where(owned, rank.astype(jnp.int32), -1)
    mark = jnp.sum(hot * (member + 1).astype(F32), axis=0, keepdims=True)
    slot_ids = lax.broadcasted_iota(jnp.int32, (capacity, rows), 0)
    loads[2].wait()
    loads[3].wait()
    fields = jnp.concatenate(
        [
            coef[...],
            data[...],
            jnp.broadcast_to(mark, (LANES - coef_rows - dates, rows)),
        ],
        axis=0,
    )
    high, low = split(fields)

    def placed(o):
        chosen = jnp.where(slot_ids == slot[o : o + 1, :], 1.0, 0.0).astype(BF16)
        return contract(chosen, high, 1, 1) + contract(chosen, low, 1, 1)

    pl.semaphore_wait(barrier, groups - 1 + shards - 1)
    row_copies = {}
    for o in far_first:
        send[o] = placed(o)
        copy = pltpu.make_async_remote_copy(
            src_ref=send.at[o],
            dst_ref=recv.at[o],
            send_sem=d_send.at[o],
            recv_sem=d_recv.at[o],
            device_id=(leaf_peers[o], shard),
            device_id_type=MESH,
        )
        copy.start()
        row_copies[o] = copy
    recv[0] = placed(0)

    for copy in loads[4:]:
        copy.wait()
    for l in range(local):
        high, low = split(dot3(split(off[l]), split(inv[l]), 1, 0))
        wide[0, l] = high
        wide[1, l] = low
    gram = []
    for i in range(top_each):
        block = split(tinv[i])
        gram.append(split(dot3(block, block, 0, 0)))
    up = []
    for l in range(local):
        found = jnp.int32(0)
        for i in range(total):
            found = jnp.where(lmap[i] == me * local + l, lpar[i], found)
        up.append(found)

    lane_group = lax.broadcasted_iota(jnp.int32, (piece, LANES), 1) // coef_rows
    forwards = []
    for g in range(pair):
        for o in range(g * per, (g + 1) * per):
            if o > 0:
                row_copies[o].wait_recv()
            block = recv[o]
            out = block[:piece]
            for q in range(1, fold):
                moved = pltpu.roll(block[q * piece : (q + 1) * piece], q * coef_rows, 1)
                out = jnp.where(lane_group == q, moved, out)
            packed[shard, o] = out
        span = pl.ds(g * per, per)
        for o in range(1, shards):
            copy = pltpu.make_async_remote_copy(
                src_ref=packed.at[shard, span],
                dst_ref=packed.at[shard, span],
                send_sem=f_send.at[o, g],
                recv_sem=f_recv.at[o, g],
                device_id=(me, rhs_peers[o]),
                device_id_type=MESH,
            )
            copy.start()
            forwards.append(copy)
    ready = len(forwards) // 2
    span = groups // 2
    big_group = lax.broadcasted_iota(jnp.int32, (span * piece, LANES), 1) // coef_rows
    rhs_all = None
    for part in range(2):
        here = slice(part * span, (part + 1) * span)
        rows_in = recv[here].reshape(span * capacity, LANES)
        turned = split(rows_in.T)
        marks = rows_in[:, coef_rows + dates : coef_rows + dates + 1]
        for copy in forwards[part * ready : (part + 1) * ready]:
            copy.wait_recv()
        packs = [packed[s, here].reshape(span * piece, LANES) for s in range(shards)]
        pieces = []
        for q in range(fold):
            out = None
            for s in range(shards):
                shift = ((s - q) * coef_rows) % LANES
                moved = pltpu.roll(packs[s], shift, 1) if shift else packs[s]
                out = moved if out is None else jnp.where(big_group == s, moved, out)
            pieces.append(out.reshape(span, 1, piece, LANES))
        coefs = jnp.concatenate(pieces, axis=1).reshape(span * capacity, LANES)
        spread = jnp.concatenate(
            [jnp.where(marks == float(l + 1), coefs, 0.0) for l in range(local)], axis=1
        )
        term = dot3(turned, split(spread), 1, 0)[coef_rows : coef_rows + dates]
        rhs_all = term if rhs_all is None else rhs_all + term
    rhs = [
        [split(rhs_all[n : n + half, l * width : (l + 1) * width]) for l in range(local)]
        for n in range(0, dates, half)
    ]
    steps = [h // 2 for h in far_first if h % 2 == 0] + [0]
    cross, sums, solutions = {}, {}, {}
    weight = [[jnp.where(up[l] == p, 1.0, 0.0) for p in range(tops_all)] for l in range(local)]
    for n in range(cuts):
        updates = [dot3(rhs[n][l], (wide[0, l], wide[1, l]), 1, 1) for l in range(local)]
        for p in range(tops_all):
            acc = weight[0][p] * updates[0]
            for l in range(1, local):
                acc = acc + weight[l][p] * updates[l]
            parts[n, p] = acc
        for h in steps:
            copy = pltpu.make_async_remote_copy(
                src_ref=parts.at[n, pl.ds(leaf_peers[2 * h + 1] * top_each, top_each)],
                dst_ref=across.at[n, h],
                send_sem=a_send.at[n, h],
                recv_sem=a_recv.at[n, h],
                device_id=(leaf_peers[1], shard),
                device_id_type=MESH,
            )
            copy.start()
            cross[n, h] = copy
    residue = []
    for n in range(cuts):
        for h in steps:
            cross[n, h].wait_recv()
            here = parts[n, pl.ds(leaf_peers[2 * h] * top_each, top_each)] + across[n, h]
            if h == 0:
                residue.append(trhs[:, n * half : (n + 1) * half] - here)
                continue
            joined[n, h] = here
            copy = pltpu.make_async_remote_copy(
                src_ref=joined.at[n, h],
                dst_ref=along.at[n, h],
                send_sem=z_send.at[n, h],
                recv_sem=z_recv.at[n, h],
                device_id=(leaf_peers[2 * h], shard),
                device_id_type=MESH,
            )
            copy.start()
            sums[n, h] = copy
    for l in range(local):
        factor = split(inv[l])
        for n in range(cuts):
            solved = split(dot3(rhs[n][l], factor, 1, 1))
            base[l, n * half : (n + 1) * half] = dot3(solved, factor, 1, 0)

    def pass_on(n, o):
        block = top_out.at[tops, pl.ds(n * half, half)]
        copy = pltpu.make_async_remote_copy(
            src_ref=block,
            dst_ref=block,
            send_sem=g_send.at[n, o],
            recv_sem=g_recv.at[n, o],
            device_id=(leaf_peers[o], shard),
            device_id_type=MESH,
        )
        copy.start()
        solutions[n, o] = copy

    for n in range(cuts):
        left = residue[n]
        for h in steps[:-1]:
            sums[n, h].wait_recv()
            left = left - along[n, h]
        for i in range(top_each):
            top_out[me * top_each + i, n * half : (n + 1) * half] = dot3(
                split(left[i]), gram[i], 1, 0
            )
        for o in far_first:
            pass_on(n, o)
    for copy in [*row_copies.values(), *forwards, *cross.values(), *sums.values()]:
        copy.wait_send()
    for n in range(cuts):
        for o in reversed(far_first):
            solutions[n, o].wait_recv()
        dates_here = slice(n * half, (n + 1) * half)
        for l in range(local):
            own = weight[l][0] * top_out[0, dates_here]
            for p in range(1, tops_all):
                own = own + weight[l][p] * top_out[p, dates_here]
            lifted = dot3(split(own), (wide[0, l], wide[1, l]), 1, 0)
            leaf_out[l, dates_here] = base[l, dates_here] - lifted
    for copy in solutions.values():
        copy.wait_send()


def write_out(leaf_v, top_v, leaf_h, top_h, sems):
    copies = [
        pltpu.make_async_copy(leaf_v, leaf_h, sems.at[0]),
        pltpu.make_async_copy(top_v, top_h, sems.at[1]),
    ]
    for copy in copies:
        copy.start()
    for copy in copies:
        copy.wait()


def fused(
    obs_coef, obs_data, obs_target, leaf_map, leaf_parent, leaf_inv, leaf_off, top_inv, top_rhs
):
    groups, shards = lax.axis_size("leaf"), lax.axis_size("rhs")
    rows = obs_target.shape[0]
    capacity = 2 * rows // groups
    local, width = leaf_inv.shape[0], leaf_inv.shape[1]
    top_count, dates = top_inv.shape[0], obs_data.shape[0]
    top_each = top_count // groups
    coef_rows = obs_coef.shape[0]
    piece = capacity * coef_rows // LANES
    pair = groups // 2
    cuts = 2 if dates % 16 == 0 else 1
    half = dates // cuts
    dma = pltpu.SemaphoreType.DMA
    vmem = pl.BlockSpec(memory_space=pltpu.VMEM)
    hbm = pl.BlockSpec(memory_space=pltpu.HBM)
    results = (
        jax.ShapeDtypeStruct((local, dates, width), F32),
        jax.ShapeDtypeStruct((top_count, dates, width), F32),
    )
    solved = pl.pallas_call(
        functools.partial(kernel, groups, shards, capacity),
        out_shape=results,
        in_specs=[hbm] * 9,
        out_specs=(vmem, vmem),
        scratch_shapes=[
            pltpu.VMEM((1, rows), jnp.int32),
            pltpu.VMEM(obs_coef.shape, F32),
            pltpu.VMEM(obs_data.shape, F32),
            pltpu.SMEM(leaf_map.shape, jnp.int32),
            pltpu.SMEM(leaf_parent.shape, jnp.int32),
            pltpu.VMEM(leaf_inv.shape, F32),
            pltpu.VMEM(leaf_off.shape, F32),
            pltpu.VMEM((top_each, width, width), F32),
            pltpu.VMEM((top_each, dates, width), F32),
            pltpu.VMEM((groups, capacity, LANES), F32),
            pltpu.VMEM((groups, capacity, LANES), F32),
            pltpu.VMEM((shards, groups, piece, LANES), F32),
            pltpu.VMEM((2, local, width, width), BF16),
            pltpu.VMEM((local, dates, width), F32),
            pltpu.VMEM((cuts, top_count, half, width), F32),
            pltpu.VMEM((cuts, groups // 2, top_each, half, width), F32),
            pltpu.VMEM((cuts, groups // 2, top_each, half, width), F32),
            pltpu.VMEM((cuts, groups // 2, top_each, half, width), F32),
            dma((groups,)),
            dma((groups,)),
            dma((shards, pair)),
            dma((shards, pair)),
            dma((cuts, groups // 2)),
            dma((cuts, groups // 2)),
            dma((cuts, groups // 2)),
            dma((cuts, groups // 2)),
            dma((cuts, groups)),
            dma((cuts, groups)),
            dma((9,)),
        ],
        compiler_params=pltpu.CompilerParams(
            collective_id=0, has_side_effects=True, vmem_limit_bytes=24 * 2**20
        ),
    )(
        *(
            pltpu.with_memory_space_constraint(x, pltpu.HBM)
            for x in (
                obs_target.reshape(1, rows), obs_coef, obs_data, leaf_map, leaf_parent,
                leaf_inv, leaf_off, top_inv, top_rhs,
            )
        )
    )
    return pl.pallas_call(
        write_out,
        out_shape=results,
        in_specs=[vmem, vmem],
        out_specs=(hbm, hbm),
        scratch_shapes=[dma((2,))],
        compiler_params=pltpu.CompilerParams(vmem_limit_bytes=4 * 2**20),
    )(*solved)


def plain(
    obs_coef, obs_data, obs_target, leaf_map, leaf_parent, leaf_inv, leaf_off, top_inv, top_rhs
):
    highest = lax.Precision.HIGHEST
    groups = lax.axis_size("leaf")
    device_index = lax.axis_index("leaf")
    local_count = leaf_inv.shape[0]
    block_width = leaf_inv.shape[1]
    top_count = top_inv.shape[0]
    date_cols = obs_data.shape[0]
    rows_here = obs_target.shape[0]
    leaf_total = leaf_map.shape[0]
    capacity = max(2, 2 * rows_here // groups)
    slots_total = groups * capacity
    all_ids = jnp.arange(leaf_total, dtype=jnp.int32)
    id_match = obs_target[:, None] == all_ids[None, :]
    position = jnp.sum(jnp.where(id_match, leaf_map[None, :], 0), axis=1)
    owner_dev = position // local_count
    member = position % local_count
    row_ids = jnp.arange(rows_here, dtype=jnp.int32)
    earlier = (owner_dev[:, None] == owner_dev[None, :]) & (row_ids[:, None] > row_ids[None, :])
    queue_rank = jnp.sum(earlier.astype(jnp.int32), axis=1)
    target_slot = owner_dev * capacity + queue_rank
    slot_mark = (member + 1).astype(jnp.float32)[None, :]
    fields = jnp.concatenate([obs_coef, obs_data, slot_mark], axis=0)
    placed = jnp.zeros((fields.shape[0], slots_total), F32).at[:, target_slot].set(fields)
    received = lax.all_to_all(placed, "leaf", split_axis=1, concat_axis=1, tiled=True)
    part_coef = received[: obs_coef.shape[0]]
    recv_data = received[obs_coef.shape[0] : -1]
    recv_mark = received[-1:]
    recv_coef = lax.all_gather(part_coef, "rhs", axis=0, tiled=True)
    slot_values = (jnp.arange(local_count, dtype=jnp.int32) + 1).astype(jnp.float32)
    chosen = (recv_mark[0][None, :] == slot_values[:, None]).astype(jnp.float32)
    spread = (recv_data[None, :, :] * chosen[:, None, :]).reshape(
        local_count * date_cols, slots_total
    )
    leaf_rhs = lax.dot_general(
        spread, recv_coef, (((1,), (1,)), ((), ())), precision=highest
    ).reshape(local_count, date_cols, block_width)
    solved = jnp.einsum("ltc,ldc->ltd", leaf_rhs, leaf_inv, precision=highest)
    update = jnp.einsum("ltd,lcd->ltc", solved, leaf_off, precision=highest)
    positions_here = device_index * local_count + jnp.arange(local_count, dtype=jnp.int32)
    holder_match = leaf_map[None, :] == positions_here[:, None]
    parent_here = jnp.sum(jnp.where(holder_match, leaf_parent[None, :], 0), axis=1)
    to_top = (parent_here[:, None] == jnp.arange(top_count, dtype=jnp.int32)[None, :]).astype(
        jnp.float32
    )
    contrib = jnp.einsum("lp,ltc->ptc", to_top, update, precision=highest)
    flat_terms = contrib.reshape(top_count * date_cols, block_width)
    top_total = lax.psum(flat_terms, "leaf").reshape(top_count, date_cols, block_width)
    residue = top_rhs - top_total
    top_solved = jnp.einsum("ptc,pdc->ptd", residue, top_inv, precision=highest)
    top_solution = jnp.einsum("ptd,pdc->ptc", top_solved, top_inv, precision=highest)
    from_top = jnp.einsum("lp,ptc->ltc", to_top, top_solution, precision=highest)
    lifted = jnp.einsum("ltc,lcd->ltd", from_top, leaf_off, precision=highest)
    leaf_solution = jnp.einsum("ltc,lcd->ltd", solved - lifted, leaf_inv, precision=highest)
    return (leaf_solution, top_solution)


def body(*args):
    obs_coef, obs_data, obs_target = args[:3]
    groups = lax.axis_size("leaf")
    coef_rows, rows = obs_coef.shape
    dates = obs_data.shape[0]
    fits = (
        args[7].shape[0] % groups == 0
        and groups > 1
        and groups & (groups - 1) == 0
        and rows % LANES == 0
        and (2 * rows) % groups == 0
        and LANES % coef_rows == 0
        and (2 * rows // groups) % (8 * (LANES // coef_rows)) == 0
        and coef_rows % 8 == 0
        and dates % 8 == 0
        and coef_rows + dates < LANES
        and args[5].shape[1] == LANES
    )
    return fused(*args) if fits else plain(*args)


def solution(mesh):
    return jax.shard_map(
        body,
        mesh=mesh,
        in_specs=(
            P("rhs", "leaf"),
            P("rhs", "leaf"),
            P("leaf"),
            P(),
            P(),
            P("leaf", None, None),
            P("leaf", None, None),
            P(),
            P(None, "rhs", None),
        ),
        out_specs=(P("leaf", "rhs", None), P(None, "rhs", None)),
        check_vma=False,
    )
```

```python
import functools

import jax
import jax.numpy as jnp
from jax import lax
from jax.experimental import pallas as pl
from jax.experimental.pallas import tpu as pltpu
from jax.sharding import PartitionSpec as P

F32, BF16 = jnp.float32, jnp.bfloat16
MESH = pl.DeviceIdType.MESH
LANES = 128


def split(x):
    high = x.astype(BF16)
    return high, (x - high.astype(F32)).astype(BF16)


def contract(a, b, ca, cb):
    return lax.dot_general(a, b, (((ca,), (cb,)), ((), ())), preferred_element_type=F32)


def dot3(a, b, ca, cb):
    (ah, al), (bh, bl) = a, b
    return contract(ah, bh, ca, cb) + (contract(ah, bl, ca, cb) + contract(al, bh, ca, cb))


def flipped(index, bits, count):
    out = index
    place = 1
    while place < count:
        if bits & place:
            out = out + place * (1 - 2 * lax.rem(lax.div(index, place), 2))
        place *= 2
    return out


def kernel(
    groups, shards, capacity,
    tgt_h, coef_h, data_h, lmap_h, lpar_h, inv_h, off_h, tinv_h, trhs_h,
    leaf_out, top_out,
    tgt, coef, data, lmap, lpar, inv, off, tinv, trhs,
    send, recv, packed, wide, base, parts, across, joined, along,
    d_send, d_recv, f_send, f_recv, a_send, a_recv, z_send, z_recv, g_send, g_recv, l_sem,
):
    me = lax.axis_index("leaf")
    shard = lax.axis_index("rhs")
    local, width = inv.shape[0], inv.shape[1]
    coef_rows, rows = coef.shape
    dates = data.shape[0]
    top_each = tinv.shape[0]
    total = lmap.shape[0]
    fold = LANES // coef_rows
    piece = capacity // fold
    pair = f_send.shape[1]
    cuts, tops_all, half = parts.shape[0], parts.shape[1], parts.shape[2]
    per = groups // pair
    leaf_peers = [flipped(me, o, groups) for o in range(groups)]
    far_first = sorted(range(1, groups), key=lambda o: (-(o.bit_length()), o))
    rhs_peers = [lax.rem(shard + o, shards) for o in range(shards)]

    barrier = pltpu.get_barrier_semaphore()
    for o in range(1, groups):
        pl.semaphore_signal(barrier, inc=1, device_id=(leaf_peers[o], shard), device_id_type=MESH)
    for o in range(1, shards):
        pl.semaphore_signal(barrier, inc=1, device_id=(me, rhs_peers[o]), device_id_type=MESH)
    tops = pl.ds(me * top_each, top_each)
    loads = []
    for i, (src, dst) in enumerate(
        [
            (tgt_h, tgt),
            (lmap_h, lmap),
            (coef_h, coef),
            (data_h, data),
            (lpar_h, lpar),
            (inv_h, inv),
            (off_h, off),
            (tinv_h.at[tops], tinv),
            (trhs_h.at[tops], trhs),
        ]
    ):
        copy = pltpu.make_async_copy(src, dst, l_sem.at[i])
        copy.start()
        loads.append(copy)
    loads[0].wait()
    loads[1].wait()

    target = tgt[...]
    position = jnp.zeros_like(target)
    for i in range(total):
        position = jnp.where(target == i, lmap[i], position)
    place = lax.broadcasted_iota(jnp.int32, (groups, rows), 0)
    first = jnp.zeros_like(place)
    for o in range(groups):
        first = jnp.where(place == o, leaf_peers[o] * local, first)
    member = jnp.broadcast_to(position, (groups, rows)) - first
    owned = (member >= 0) & (member < local)
    hot = jnp.where(owned, 1.0, 0.0)
    before = (
        lax.broadcasted_iota(jnp.int32, (rows, rows), 0)
        < lax.broadcasted_iota(jnp.int32, (rows, rows), 1)
    )
    rank = contract(hot.astype(BF16), jnp.where(before, 1.0, 0.0).astype(BF16), 1, 0)
    slot = jnp.where(owned, rank.astype(jnp.int32), -1)
    mark = jnp.sum(hot * (member + 1).astype(F32), axis=0, keepdims=True)
    slot_ids = lax.broadcasted_iota(jnp.int32, (capacity, rows), 0)
    loads[2].wait()
    loads[3].wait()
    fields = jnp.concatenate(
        [
            coef[...],
            data[...],
            jnp.broadcast_to(mark, (LANES - coef_rows - dates, rows)),
        ],
        axis=0,
    )
    high, low = split(fields)

    def placed(o):
        chosen = jnp.where(slot_ids == slot[o : o + 1, :], 1.0, 0.0).astype(BF16)
        return contract(chosen, high, 1, 1) + contract(chosen, low, 1, 1)

    pl.semaphore_wait(barrier, groups - 1 + shards - 1)
    row_copies = {}
    for o in far_first:
        send[o] = placed(o)
        copy = pltpu.make_async_remote_copy(
            src_ref=send.at[o],
            dst_ref=recv.at[o],
            send_sem=d_send.at[o],
            recv_sem=d_recv.at[o],
            device_id=(leaf_peers[o], shard),
            device_id_type=MESH,
        )
        copy.start()
        row_copies[o] = copy
    recv[0] = placed(0)

    for copy in loads[4:]:
        copy.wait()
    for l in range(local):
        high, low = split(dot3(split(off[l]), split(inv[l]), 1, 0))
        wide[0, l] = high
        wide[1, l] = low
    gram = []
    for i in range(top_each):
        block = split(tinv[i])
        gram.append(split(dot3(block, block, 0, 0)))
    up = []
    for l in range(local):
        found = jnp.int32(0)
        for i in range(total):
            found = jnp.where(lmap[i] == me * local + l, lpar[i], found)
        up.append(found)

    lane_group = lax.broadcasted_iota(jnp.int32, (piece, LANES), 1) // coef_rows
    forwards = []
    for g in range(pair):
        for o in range(g * per, (g + 1) * per):
            if o > 0:
                row_copies[o].wait_recv()
            block = recv[o]
            out = block[:piece]
            for q in range(1, fold):
                moved = pltpu.roll(block[q * piece : (q + 1) * piece], q * coef_rows, 1)
                out = jnp.where(lane_group == q, moved, out)
            packed[shard, o] = out
        span = pl.ds(g * per, per)
        for o in range(1, shards):
            copy = pltpu.make_async_remote_copy(
                src_ref=packed.at[shard, span],
                dst_ref=packed.at[shard, span],
                send_sem=f_send.at[o, g],
                recv_sem=f_recv.at[o, g],
                device_id=(me, rhs_peers[o]),
                device_id_type=MESH,
            )
            copy.start()
            forwards.append(copy)
    ready = len(forwards) // 2
    span = groups // 2
    big_group = lax.broadcasted_iota(jnp.int32, (span * piece, LANES), 1) // coef_rows
    rhs_all = None
    for part in range(2):
        here = slice(part * span, (part + 1) * span)
        rows_in = recv[here].reshape(span * capacity, LANES)
        turned = split(rows_in.T)
        marks = rows_in[:, coef_rows + dates : coef_rows + dates + 1]
        for copy in forwards[part * ready : (part + 1) * ready]:
            copy.wait_recv()
        packs = [packed[s, here].reshape(span * piece, LANES) for s in range(shards)]
        pieces = []
        for q in range(fold):
            out = None
            for s in range(shards):
                shift = ((s - q) * coef_rows) % LANES
                moved = pltpu.roll(packs[s], shift, 1) if shift else packs[s]
                out = moved if out is None else jnp.where(big_group == s, moved, out)
            pieces.append(out.reshape(span, 1, piece, LANES))
        coefs = jnp.concatenate(pieces, axis=1).reshape(span * capacity, LANES)
        spread = jnp.concatenate(
            [jnp.where(marks == float(l + 1), coefs, 0.0) for l in range(local)], axis=1
        )
        term = dot3(turned, split(spread), 1, 0)[coef_rows : coef_rows + dates]
        rhs_all = term if rhs_all is None else rhs_all + term
    rhs = [
        [split(rhs_all[n : n + half, l * width : (l + 1) * width]) for l in range(local)]
        for n in range(0, dates, half)
    ]
    steps = [h // 2 for h in far_first if h % 2 == 0] + [0]
    cross, sums, solutions = {}, {}, {}
    weight = [[jnp.where(up[l] == p, 1.0, 0.0) for p in range(tops_all)] for l in range(local)]
    for n in range(cuts):
        updates = [dot3(rhs[n][l], (wide[0, l], wide[1, l]), 1, 1) for l in range(local)]
        for p in range(tops_all):
            acc = weight[0][p] * updates[0]
            for l in range(1, local):
                acc = acc + weight[l][p] * updates[l]
            parts[n, p] = acc
        for h in steps:
            copy = pltpu.make_async_remote_copy(
                src_ref=parts.at[n, pl.ds(leaf_peers[2 * h + 1] * top_each, top_each)],
                dst_ref=across.at[n, h],
                send_sem=a_send.at[n, h],
                recv_sem=a_recv.at[n, h],
                device_id=(leaf_peers[1], shard),
                device_id_type=MESH,
            )
            copy.start()
            cross[n, h] = copy
    residue = []
    for n in range(cuts):
        for h in steps:
            cross[n, h].wait_recv()
            here = parts[n, pl.ds(leaf_peers[2 * h] * top_each, top_each)] + across[n, h]
            if h == 0:
                residue.append(trhs[:, n * half : (n + 1) * half] - here)
                continue
            joined[n, h] = here
            copy = pltpu.make_async_remote_copy(
                src_ref=joined.at[n, h],
                dst_ref=along.at[n, h],
                send_sem=z_send.at[n, h],
                recv_sem=z_recv.at[n, h],
                device_id=(leaf_peers[2 * h], shard),
                device_id_type=MESH,
            )
            copy.start()
            sums[n, h] = copy
    def leaf_part(n):
        for l in range(local):
            factor = split(inv[l])
            solved = split(dot3(rhs[n][l], factor, 1, 1))
            base[l, n * half : (n + 1) * half] = dot3(solved, factor, 1, 0)

    leaf_part(0)

    def pass_on(n, h, o, peer):
        block = top_out.at[pl.ds(leaf_peers[h] * top_each, top_each), pl.ds(n * half, half)]
        copy = pltpu.make_async_remote_copy(
            src_ref=block,
            dst_ref=block,
            send_sem=g_send.at[n, o],
            recv_sem=g_recv.at[n, o],
            device_id=(leaf_peers[peer], shard),
            device_id_type=MESH,
        )
        copy.start()
        solutions[n, o] = copy

    for n in range(cuts):
        left = residue[n]
        for h in steps[:-1]:
            sums[n, h].wait_recv()
            left = left - along[n, h]
        for i in range(top_each):
            top_out[me * top_each + i, n * half : (n + 1) * half] = dot3(
                split(left[i]), gram[i], 1, 0
            )
        pass_on(n, 0, 1, 1)
        for h in steps[:-1]:
            pass_on(n, 0, 2 * h, 2 * h)
    for n in range(cuts):
        for h in reversed(steps[:-1]):
            solutions[n, 2 * h].wait_recv()
            pass_on(n, 2 * h, 2 * h + 1, 1)
    for n in range(1, cuts):
        leaf_part(n)
    for copy in [*row_copies.values(), *forwards, *cross.values(), *sums.values()]:
        copy.wait_send()
    for n in range(cuts):
        for h in reversed(steps):
            solutions[n, 2 * h + 1].wait_recv()
        dates_here = slice(n * half, (n + 1) * half)
        for l in range(local):
            own = weight[l][0] * top_out[0, dates_here]
            for p in range(1, tops_all):
                own = own + weight[l][p] * top_out[p, dates_here]
            lifted = dot3(split(own), (wide[0, l], wide[1, l]), 1, 0)
            leaf_out[l, dates_here] = base[l, dates_here] - lifted
    for copy in solutions.values():
        copy.wait_send()


def write_out(leaf_v, top_v, leaf_h, top_h, sems):
    copies = [
        pltpu.make_async_copy(leaf_v, leaf_h, sems.at[0]),
        pltpu.make_async_copy(top_v, top_h, sems.at[1]),
    ]
    for copy in copies:
        copy.start()
    for copy in copies:
        copy.wait()


def fused(
    obs_coef, obs_data, obs_target, leaf_map, leaf_parent, leaf_inv, leaf_off, top_inv, top_rhs
):
    groups, shards = lax.axis_size("leaf"), lax.axis_size("rhs")
    rows = obs_target.shape[0]
    capacity = 2 * rows // groups
    local, width = leaf_inv.shape[0], leaf_inv.shape[1]
    top_count, dates = top_inv.shape[0], obs_data.shape[0]
    top_each = top_count // groups
    coef_rows = obs_coef.shape[0]
    piece = capacity * coef_rows // LANES
    pair = groups // 2
    cuts = 2 if dates % 16 == 0 else 1
    half = dates // cuts
    dma = pltpu.SemaphoreType.DMA
    vmem = pl.BlockSpec(memory_space=pltpu.VMEM)
    hbm = pl.BlockSpec(memory_space=pltpu.HBM)
    results = (
        jax.ShapeDtypeStruct((local, dates, width), F32),
        jax.ShapeDtypeStruct((top_count, dates, width), F32),
    )
    solved = pl.pallas_call(
        functools.partial(kernel, groups, shards, capacity),
        out_shape=results,
        in_specs=[hbm] * 9,
        out_specs=(vmem, vmem),
        scratch_shapes=[
            pltpu.VMEM((1, rows), jnp.int32),
            pltpu.VMEM(obs_coef.shape, F32),
            pltpu.VMEM(obs_data.shape, F32),
            pltpu.SMEM(leaf_map.shape, jnp.int32),
            pltpu.SMEM(leaf_parent.shape, jnp.int32),
            pltpu.VMEM(leaf_inv.shape, F32),
            pltpu.VMEM(leaf_off.shape, F32),
            pltpu.VMEM((top_each, width, width), F32),
            pltpu.VMEM((top_each, dates, width), F32),
            pltpu.VMEM((groups, capacity, LANES), F32),
            pltpu.VMEM((groups, capacity, LANES), F32),
            pltpu.VMEM((shards, groups, piece, LANES), F32),
            pltpu.VMEM((2, local, width, width), BF16),
            pltpu.VMEM((local, dates, width), F32),
            pltpu.VMEM((cuts, top_count, half, width), F32),
            pltpu.VMEM((cuts, groups // 2, top_each, half, width), F32),
            pltpu.VMEM((cuts, groups // 2, top_each, half, width), F32),
            pltpu.VMEM((cuts, groups // 2, top_each, half, width), F32),
            dma((groups,)),
            dma((groups,)),
            dma((shards, pair)),
            dma((shards, pair)),
            dma((cuts, groups // 2)),
            dma((cuts, groups // 2)),
            dma((cuts, groups // 2)),
            dma((cuts, groups // 2)),
            dma((cuts, groups)),
            dma((cuts, groups)),
            dma((9,)),
        ],
        compiler_params=pltpu.CompilerParams(
            collective_id=0, has_side_effects=True, vmem_limit_bytes=24 * 2**20
        ),
    )(
        *(
            pltpu.with_memory_space_constraint(x, pltpu.HBM)
            for x in (
                obs_target.reshape(1, rows), obs_coef, obs_data, leaf_map, leaf_parent,
                leaf_inv, leaf_off, top_inv, top_rhs,
            )
        )
    )
    return pl.pallas_call(
        write_out,
        out_shape=results,
        in_specs=[vmem, vmem],
        out_specs=(hbm, hbm),
        scratch_shapes=[dma((2,))],
        compiler_params=pltpu.CompilerParams(vmem_limit_bytes=4 * 2**20),
    )(*solved)


def plain(
    obs_coef, obs_data, obs_target, leaf_map, leaf_parent, leaf_inv, leaf_off, top_inv, top_rhs
):
    highest = lax.Precision.HIGHEST
    groups = lax.axis_size("leaf")
    device_index = lax.axis_index("leaf")
    local_count = leaf_inv.shape[0]
    block_width = leaf_inv.shape[1]
    top_count = top_inv.shape[0]
    date_cols = obs_data.shape[0]
    rows_here = obs_target.shape[0]
    leaf_total = leaf_map.shape[0]
    capacity = max(2, 2 * rows_here // groups)
    slots_total = groups * capacity
    all_ids = jnp.arange(leaf_total, dtype=jnp.int32)
    id_match = obs_target[:, None] == all_ids[None, :]
    position = jnp.sum(jnp.where(id_match, leaf_map[None, :], 0), axis=1)
    owner_dev = position // local_count
    member = position % local_count
    row_ids = jnp.arange(rows_here, dtype=jnp.int32)
    earlier = (owner_dev[:, None] == owner_dev[None, :]) & (row_ids[:, None] > row_ids[None, :])
    queue_rank = jnp.sum(earlier.astype(jnp.int32), axis=1)
    target_slot = owner_dev * capacity + queue_rank
    slot_mark = (member + 1).astype(jnp.float32)[None, :]
    fields = jnp.concatenate([obs_coef, obs_data, slot_mark], axis=0)
    placed = jnp.zeros((fields.shape[0], slots_total), F32).at[:, target_slot].set(fields)
    received = lax.all_to_all(placed, "leaf", split_axis=1, concat_axis=1, tiled=True)
    part_coef = received[: obs_coef.shape[0]]
    recv_data = received[obs_coef.shape[0] : -1]
    recv_mark = received[-1:]
    recv_coef = lax.all_gather(part_coef, "rhs", axis=0, tiled=True)
    slot_values = (jnp.arange(local_count, dtype=jnp.int32) + 1).astype(jnp.float32)
    chosen = (recv_mark[0][None, :] == slot_values[:, None]).astype(jnp.float32)
    spread = (recv_data[None, :, :] * chosen[:, None, :]).reshape(
        local_count * date_cols, slots_total
    )
    leaf_rhs = lax.dot_general(
        spread, recv_coef, (((1,), (1,)), ((), ())), precision=highest
    ).reshape(local_count, date_cols, block_width)
    solved = jnp.einsum("ltc,ldc->ltd", leaf_rhs, leaf_inv, precision=highest)
    update = jnp.einsum("ltd,lcd->ltc", solved, leaf_off, precision=highest)
    positions_here = device_index * local_count + jnp.arange(local_count, dtype=jnp.int32)
    holder_match = leaf_map[None, :] == positions_here[:, None]
    parent_here = jnp.sum(jnp.where(holder_match, leaf_parent[None, :], 0), axis=1)
    to_top = (parent_here[:, None] == jnp.arange(top_count, dtype=jnp.int32)[None, :]).astype(
        jnp.float32
    )
    contrib = jnp.einsum("lp,ltc->ptc", to_top, update, precision=highest)
    flat_terms = contrib.reshape(top_count * date_cols, block_width)
    top_total = lax.psum(flat_terms, "leaf").reshape(top_count, date_cols, block_width)
    residue = top_rhs - top_total
    top_solved = jnp.einsum("ptc,pdc->ptd", residue, top_inv, precision=highest)
    top_solution = jnp.einsum("ptd,pdc->ptc", top_solved, top_inv, precision=highest)
    from_top = jnp.einsum("lp,ptc->ltc", to_top, top_solution, precision=highest)
    lifted = jnp.einsum("ltc,lcd->ltd", from_top, leaf_off, precision=highest)
    leaf_solution = jnp.einsum("ltc,lcd->ltd", solved - lifted, leaf_inv, precision=highest)
    return (leaf_solution, top_solution)


def body(*args):
    obs_coef, obs_data, obs_target = args[:3]
    groups = lax.axis_size("leaf")
    coef_rows, rows = obs_coef.shape
    dates = obs_data.shape[0]
    fits = (
        args[7].shape[0] % groups == 0
        and groups > 1
        and groups & (groups - 1) == 0
        and rows % LANES == 0
        and (2 * rows) % groups == 0
        and LANES % coef_rows == 0
        and (2 * rows // groups) % (8 * (LANES // coef_rows)) == 0
        and coef_rows % 8 == 0
        and dates % 8 == 0
        and coef_rows + dates < LANES
        and args[5].shape[1] == LANES
    )
    return fused(*args) if fits else plain(*args)


def solution(mesh):
    return jax.shard_map(
        body,
        mesh=mesh,
        in_specs=(
            P("rhs", "leaf"),
            P("rhs", "leaf"),
            P("leaf"),
            P(),
            P(),
            P("leaf", None, None),
            P("leaf", None, None),
            P(),
            P(None, "rhs", None),
        ),
        out_specs=(P("leaf", "rhs", None), P(None, "rhs", None)),
        check_vma=False,
    )
```
